32 devices in a mesh: dp: 8 (over y, x, core), mp: 4 (over z).
Axes of the slice: x: 2, y: 2, z: 4, core: 2. Of those that a mesh axis runs over, the one named last changes fastest.
Arguments:
- item_ids: int32 [4, 3072], P(None, 'dp'), may hold values from 0 to 36863
- session_ends: int32 [3, 3072], P(None, 'dp'), may hold values 0 or 1
- negatives: int32 [2048], replicated, may hold values from 0 to 36863
- embedding: bfloat16 [1000, 36864], P('mp'), may hold values from -6 to 6
- in_weight: bfloat16 [3, 1000, 1000], P(None, None, 'mp'), may hold values from -0.1875 to 0.1875
- hid_weight: bfloat16 [3, 1000, 1000], P(None, None, 'mp'), may hold values from -0.1875 to 0.1875
- gate_bias: float32 [3, 1000], P(None, 'mp'), may hold values from -3 to 3
- cand_bias: float32 [1000], P('mp'), may hold values from -3 to 3
- out_table: bfloat16 [1000, 36864], P('mp'), may hold values from -0.75 to 0.75
- out_bias: float32 [36864], replicated, may hold values from -6 to 6
Outputs:
- loss: float32 [], replicated
- in_weight_grad: float32 [3, 1000, 1000], P(None, None, 'mp')
- hid_weight_grad: float32 [3, 1000, 1000], P(None, None, 'mp')
- gate_bias_grad: float32 [3, 1000], P(None, 'mp')
- cand_bias_grad: float32 [1000], P('mp')
- embedding_grad: float32 [1000, 36864], P('mp', 'dp')
- out_table_grad: float32 [1000, 36864], P('mp', 'dp')
- out_bias_grad: float32 [36864], P('dp')
The draws below stay inside these ranges and needn't reach their ends.
All inputs are finite; a program needn't handle non-finite values. No bound on the sum of `session_ends` on one device may be relied on, other than what follows from the above.
Results may differ from the reference program's by a relative error of at most 0.0017.
Values may be sent and summed in bfloat16 or wider, within the bound.
No kernel may reach another device: no remote copies, remote signals or barrier semaphores. Data moves between devices by JAX's collectives and lax.ppermute only.
A program may use at most 384 MiB of HBM per device.

```python
import math
import jax
import jax.numpy as jnp
import numpy as np
from jax import lax

E = 1000
H = 1000
VOCAB = 36864
NEG = 2048
STEPS = 3
SLOTS = 3072


def set_ends(values, rng, least, top_value):
    longest = values.shape.index(max(values.shape))
    spots = []
    for shift in (0, 1):
        where = [jax.random.randint(jax.random.fold_in(rng, axis), (), 0, length) for axis, length in enumerate(values.shape)]
        where[longest] = (where[longest] + shift) % values.shape[longest]
        spots.append(tuple(where))
    return values.at[spots[0]].set(least).at[spots[1]].set(top_value)


def block_scale(key, extent, split, least, top_value):
    factor_of = 1.0
    for position, parts in split:
        heights = jax.random.uniform(jax.random.fold_in(jax.random.fold_in(key, 6), position), (parts,), jnp.float32, least / len(split), top_value / len(split))
        factor_of = factor_of * jnp.repeat(jnp.exp(heights), extent[position] // parts).reshape((-1,) + (1,) * (len(extent) - 1 - position))
    return factor_of


def rank_table(number_of, slope):
    portions = [(1 << 20) // math.isqrt(rank ** slope) + 1 for rank in range(1, number_of + 1)]
    width = 1 + sum(portions) // (1 << 30)
    return np.cumsum(np.array([max(1, weight // width) for weight in portions]))


def ranked_ids(rng, extent, amount, slope):
    grid = rank_table(amount, slope)
    ticket = jax.random.randint(jax.random.fold_in(rng, 1), extent, 0, int(grid[amount - 1]))
    rank = jnp.searchsorted(jnp.asarray(grid, jnp.int32), ticket, side="right")
    return jax.random.permutation(jax.random.fold_in(rng, 2), amount)[rank].astype(jnp.int32)


def scatter_about(stream_key, shape, width, limit, shards=(), dtype=jnp.bfloat16):
    factor_of = block_scale(stream_key, shape, shards, -0.22, 0.18) if shards else 1.0
    drawn = jax.random.normal(stream_key, shape, jnp.float32) * width * factor_of
    return jnp.minimum(jnp.maximum(drawn, -limit), limit).astype(dtype)


def setup_inputs(seed: int = 0) -> dict:
    seeds = jax.random.split(jax.random.key(seed), 11)
    return {
        "item_ids": set_ends(ranked_ids(seeds[0], (STEPS + 1, SLOTS), VOCAB, 2), jax.random.fold_in(seeds[0], 3), 0, VOCAB - 1).astype(jnp.int32),
        "session_ends": set_ends((jax.random.randint(seeds[1], (STEPS, SLOTS), 0, 8) < 1).astype(jnp.int32), jax.random.fold_in(seeds[1], 1), 0, 1),
        "negatives": set_ends(jax.random.randint(seeds[2], (NEG,), 0, VOCAB), jax.random.fold_in(seeds[2], 1), 0, VOCAB - 1).astype(jnp.int32),
        "embedding": scatter_about(seeds[3], (E, VOCAB), 1.0, 6.0, ((0, 4),)),
        "in_weight": scatter_about(seeds[4], (3, E, H), E ** -0.5, 0.1875, ((2, 4),)),
        "hid_weight": scatter_about(seeds[5], (3, H, H), H ** -0.5, 0.1875, ((2, 4),)),
        "gate_bias": scatter_about(seeds[6], (3, H), 0.5, 3.0, ((1, 4),), jnp.float32),
        "cand_bias": scatter_about(seeds[7], (H,), 0.5, 3.0, ((0, 4),), jnp.float32),
        "out_table": scatter_about(seeds[8], (H, VOCAB), 0.12, 0.75, ((0, 4),)),
        "out_bias": scatter_about(seeds[9], (VOCAB,), 1.0, 6.0, (), jnp.float32),
    }


@jax.custom_vjp
def low(v):
    return lax.optimization_barrier(v.astype(jnp.bfloat16)).astype(jnp.float32)

@jax.custom_vjp
def low_back(v):
    return v

def low_keep(v):
    return (low(v), None)

def low_pass(kept, grad):
    return (grad,)

def back_keep(v):
    return (v, None)

def back_low(kept, grad):
    return (low(grad),)
low.defvjp(low_keep, low_pass)
low_back.defvjp(back_keep, back_low)
bpr_weight = 1.0
highest = lax.Precision.HIGHEST

def reference(item_ids, session_ends, negatives, embedding, in_weight, hid_weight, gate_bias, cand_bias, out_table, out_bias):
    end_float = session_ends.astype(jnp.float32)
    starts = jnp.concatenate([jnp.ones((1, SLOTS), jnp.float32), end_float[:-1]], axis=0)
    keep_mask = 1.0 - starts
    valid_weight = (1.0 - end_float) / (STEPS * SLOTS)
    sources = item_ids[:-1]
    targets = item_ids[1:]

    def forward(table_in, weight_in, weight_hid, bias_gate, bias_cand, table_out, bias_out):
        flat_in = jnp.transpose(weight_in, (1, 0, 2)).reshape(E, 3 * H)
        flat_hid = jnp.transpose(weight_hid, (1, 0, 2)).reshape(H, 3 * H)
        neg_cols = jnp.take(table_out, negatives, axis=1)
        neg_bias = bias_out[negatives]

        def event_step(hidden, pieces):
            ids_now, tgt_now, keep_now, weight_now = pieces
            embedded = jnp.take(table_in, ids_now, axis=1).T
            from_input = low_back(jnp.dot(embedded, flat_in, precision=highest, preferred_element_type=jnp.float32)).reshape(SLOTS, 3, H)
            previous = hidden * keep_now[:, None]
            from_state = low_back(jnp.dot(low(previous), flat_hid, precision=highest, preferred_element_type=jnp.float32)).reshape(SLOTS, 3, H)
            update = jax.nn.sigmoid(from_input[:, 0] + from_state[:, 0] + bias_gate[0])
            reset_gate = jax.nn.sigmoid(from_input[:, 1] + from_state[:, 1] + bias_gate[1])
            candidate = jnp.tanh(from_input[:, 2] + bias_gate[2] + reset_gate * (from_state[:, 2] + bias_cand))
            fresh_state = (1.0 - update) * previous + update * candidate
            shown_state = low(fresh_state)
            neg_scores = low_back(jnp.dot(shown_state, neg_cols, precision=highest, preferred_element_type=jnp.float32) + neg_bias[None, :])
            tgt_cols = jnp.take(table_out, tgt_now, axis=1).T
            tgt_scores = low_back(lax.optimization_barrier(jnp.sum(shown_state * tgt_cols, axis=1)) + bias_out[tgt_now])
            weights = jax.nn.softmax(neg_scores, axis=1)
            above_prob = jax.nn.sigmoid(tgt_scores[:, None] - neg_scores)
            mixture = lax.optimization_barrier(jnp.sum(weights * above_prob, axis=1))
            spread = lax.optimization_barrier(jnp.sum(weights * neg_scores * neg_scores, axis=1))
            per_event = -jnp.log(mixture) + bpr_weight * spread
            return (fresh_state, jnp.sum(weight_now * per_event))
        start_state = jnp.zeros((SLOTS, H), jnp.float32)
        _, losses = lax.scan(jax.checkpoint(event_step), start_state, (sources, targets, keep_mask, valid_weight))
        return jnp.sum(losses)
    primals = (embedding.astype(jnp.float32), in_weight.astype(jnp.float32), hid_weight.astype(jnp.float32), gate_bias, cand_bias, out_table.astype(jnp.float32), out_bias)
    loss_value, backward = jax.vjp(forward, *primals)
    grads = backward(jnp.float32(1.0))
    return (loss_value, grads[1], grads[2], grads[3], grads[4], grads[0], grads[5], grads[6])
```

```python
import functools

import jax
import jax.numpy as jnp
from jax import lax
from jax.experimental import pallas as pl
from jax.experimental.pallas import tpu as pltpu
from jax.sharding import PartitionSpec as P

bpr_weight = 1.0
BF = jnp.bfloat16
F32 = jnp.float32
ITEM_BLOCK = 4096
CHUNK = 256
MIB = 1024 * 1024


def up(count, unit):
    return -(-count // unit) * unit


def lookup_kernel(has_bias, feats, cnt_ref, idr_ref, idc_ref, tab_ref, *rest):
    if has_bias:
        bias_ref, out_ref, perm, sid, xs, held, sems = rest
    else:
        out_ref, perm, sid, xs, held, sems = rest
    count = idr_ref.shape[1]
    blocks, _, width = held.shape

    def fetch(b):
        return pltpu.make_async_copy(
            tab_ref.at[:, pl.ds(b * width, width)], held.at[b], sems.at[b]
        )

    for b in range(blocks):
        fetch(b).start()
    lane = lax.broadcasted_iota(jnp.int32, (CHUNK, count), 1)
    keyr = idr_ref[...] * 4096 + lax.broadcasted_iota(jnp.int32, (1, count), 1)
    sid[...] = jnp.zeros_like(sid)

    def sort_rows(i, _):
        rows = pl.ds(pl.multiple_of(i * CHUNK, CHUNK), CHUNK)
        idc = idc_ref[rows, :]
        keyc = idc * 4096 + i * CHUNK + lax.broadcasted_iota(jnp.int32, (CHUNK, 1), 0)
        rank = jnp.sum((keyr < keyc).astype(F32), axis=1, keepdims=True).astype(jnp.int32)
        hit = rank == lane
        perm[rows, :] = hit.astype(F32).astype(BF)
        sid[...] += jnp.sum(jnp.where(hit, idc, 0).astype(F32), axis=0, keepdims=True)
        return 0

    lax.fori_loop(0, count // CHUNK, sort_rows, 0)
    xs[...] = jnp.zeros_like(xs)
    for b in range(blocks):
        fetch(b).wait()
        base = b * width

        def pick_chunk(c, _, b=b, base=base):
            cols = pl.ds(pl.multiple_of(c * CHUNK, CHUNK), CHUNK)
            ids = sid[:, cols].astype(jnp.int32) - base
            pick = (lax.broadcasted_iota(jnp.int32, (width, CHUNK), 0) == ids).astype(F32).astype(BF)
            xs[0:feats, cols] += jnp.dot(held[b], pick, preferred_element_type=F32)
            if has_bias:
                low = feats // 8 * 8
                value = bias_ref[:, base : base + width]
                first = value.astype(BF).astype(F32)
                second = (value - first).astype(BF).astype(F32)
                third = value - first - second
                row = lax.broadcasted_iota(jnp.int32, (8, width), 0) - (feats - low)
                parts = jnp.where(
                    row == 0, first, jnp.where(row == 1, second, jnp.where(row == 2, third, 0.0))
                ).astype(BF)
                xs[low : low + 8, cols] += jnp.dot(parts, pick, preferred_element_type=F32)
            return 0

        lax.fori_loop(
            cnt_ref[b] // CHUNK, (cnt_ref[b + 1] + CHUNK - 1) // CHUNK, pick_chunk, 0
        )
    out_ref[...] = lax.dot_general(
        perm[...], xs[...].astype(BF), (((1,), (1,)), ((), ())), preferred_element_type=F32
    ).astype(BF)


def lookup(ids, table, bias=None):
    feats, vocab = table.shape
    width = up(feats, 128)
    count = ids.shape[0]
    padded = up(count, CHUNK)
    ids = jnp.concatenate([ids, jnp.full((padded - count,), vocab, jnp.int32)])
    blocks = vocab // ITEM_BLOCK
    edges = jnp.arange(blocks + 1, dtype=jnp.int32) * ITEM_BLOCK
    cnt = jnp.sum((ids[None, :] < edges[:, None]).astype(jnp.int32), axis=1)
    vmem = pl.BlockSpec(memory_space=pltpu.VMEM)
    in_specs = [pl.BlockSpec(memory_space=pltpu.SMEM), vmem, vmem, pl.BlockSpec(memory_space=pl.ANY)]
    args = [cnt, ids.reshape(1, padded), ids.reshape(padded, 1), table]
    if bias is not None:
        in_specs.append(vmem)
        args.append(bias.reshape(1, vocab))
    return pl.pallas_call(
        functools.partial(lookup_kernel, bias is not None, feats),
        in_specs=in_specs,
        out_specs=vmem,
        scratch_shapes=[
            pltpu.VMEM((padded, padded), BF),
            pltpu.VMEM((1, padded), F32),
            pltpu.VMEM((width, padded), F32),
            pltpu.VMEM((blocks, feats, ITEM_BLOCK), BF),
            pltpu.SemaphoreType.DMA((blocks,)),
        ],
        out_shape=jax.ShapeDtypeStruct((padded, width), BF),
        compiler_params=pltpu.CompilerParams(vmem_limit_bytes=56 * MIB),
        cost_estimate=pl.CostEstimate(
            flops=2 * vocab * feats * 512, bytes_accessed=vocab * feats * 2, transcendentals=0
        ),
    )(*args)


def scatter_kernel(feats, tile, plan, base_ref, *refs):
    out_ref = refs[-1]
    first = base_ref[0] + pl.program_id(0) * tile
    out_ref[...] = jnp.zeros_like(out_ref)

    def add(piece, spot):
        out_ref[...] += lax.dot_general(
            piece, spot, (((0,), (0,)), ((), ())), preferred_element_type=F32
        )

    for ref, kind in zip(refs, plan):
        count, depth, _ = ref.shape

        def coded(part, _, ref=ref, depth=depth):
            wide = ref[part].astype(F32)
            ids = wide[:, feats + 1 : feats + 2] * 256.0 + wide[:, feats + 2 : feats + 3]
            lanes = lax.broadcasted_iota(jnp.int32, (depth, tile), 1)
            spot = jnp.where(lanes == ids.astype(jnp.int32) - first, wide[:, feats : feats + 1], 0.0)
            col = lax.broadcasted_iota(jnp.int32, wide.shape, 1)
            add(jnp.where(col == feats, 1.0, wide).astype(BF), spot.astype(BF))
            return 0

        def plain(part, _, ref=ref, depth=depth):
            rows = ref[part]
            ids = rows[:, feats + 1 : feats + 2].astype(jnp.int32) - first
            lanes = lax.broadcasted_iota(jnp.int32, (depth, tile), 1)
            spot = (lanes == ids).astype(F32).astype(BF)
            high = rows.astype(BF)
            add(high, spot)
            add((rows - high.astype(F32)).astype(BF), spot)
            return 0

        lax.fori_loop(0, count, coded if kind == "coded" else plain, 0)


def scatter(base, feats, items, arrays, plan):
    width = arrays[0].shape[-1]
    rows = sum(a.shape[0] * a.shape[1] * (1 if k == "coded" else 2) for a, k in zip(arrays, plan))
    tile = 512 if items % 512 == 0 else 128
    return pl.pallas_call(
        functools.partial(scatter_kernel, feats, tile, plan),
        grid=(items // tile,),
        in_specs=[pl.BlockSpec(memory_space=pltpu.SMEM)]
        + [pl.BlockSpec(memory_space=pltpu.VMEM)] * len(arrays),
        out_specs=pl.BlockSpec((width, tile), lambda i: (0, i)),
        out_shape=jax.ShapeDtypeStruct((width, items), F32),
        compiler_params=pltpu.CompilerParams(vmem_limit_bytes=56 * MIB),
        cost_estimate=pl.CostEstimate(
            flops=2 * rows * width * items, bytes_accessed=rows * width * 2, transcendentals=0
        ),
    )(base, *arrays)


def place_kernel(axis, where_ref, *refs):
    *pieces, out_ref, sems = refs
    copies = []
    for k, piece in enumerate(pieces):
        size = piece.shape[axis]
        spot = pl.ds(pl.multiple_of(where_ref[k] * size, size), size)
        target = out_ref.at[spot, :] if axis == 0 else out_ref.at[:, spot]
        copies.append(pltpu.make_async_copy(piece, target, sems.at[k]))
    for copy in copies:
        copy.start()
    for copy in copies:
        copy.wait()


def place(pieces, where, axis):
    shape = list(pieces[0].shape)
    shape[axis] *= len(pieces)
    anywhere = pl.BlockSpec(memory_space=pl.ANY)
    return pl.pallas_call(
        functools.partial(place_kernel, axis),
        in_specs=[pl.BlockSpec(memory_space=pltpu.SMEM)] + [anywhere] * len(pieces),
        out_specs=anywhere,
        scratch_shapes=[pltpu.SemaphoreType.DMA((len(pieces),))],
        out_shape=jax.ShapeDtypeStruct(tuple(shape), pieces[0].dtype),
        cost_estimate=pl.CostEstimate(
            flops=0, bytes_accessed=2 * sum(p.size * p.dtype.itemsize for p in pieces), transcendentals=0
        ),
    )(where, *pieces)


def swap(value, k, axis):
    count = lax.axis_size(axis)
    return lax.ppermute(value, axis, [(i, i ^ k) for i in range(count)])


def gather_mp(value):
    count = lax.axis_size("mp")
    pieces = [value] + [swap(value, k, "mp") for k in range(1, count)]
    where = lax.axis_index("mp") ^ jnp.arange(count, dtype=jnp.int32)
    return place(pieces, where, 1)


def gather_dp(value):
    count = lax.axis_size("dp")
    chips = [value] + [swap(value, k, "dp") for k in range(2, count, 2)]
    other = [swap(piece, 1, "dp") for piece in chips]
    return [piece for pair in zip(chips, other) for piece in pair]


def reduce_dp(blocks):
    kept, sent = blocks[0::2], blocks[1::2]
    got = swap(jnp.concatenate(sent), 1, "dp").reshape((len(kept),) + kept[0].shape)
    mine = [block + got[i] for i, block in enumerate(kept)]
    total = mine[0]
    for i in range(1, len(mine)):
        total = total + swap(mine[i], 2 * i, "dp")
    return total


def low(value):
    return lax.reduce_precision(value, 8, 7).astype(BF)


def on_device(
    item_ids,
    session_ends,
    negatives,
    embedding,
    in_weight,
    hid_weight,
    gate_bias,
    cand_bias,
    out_table,
    out_bias,
):
    dp, mp = lax.axis_size("dp"), lax.axis_size("mp")
    me_dp, me_mp = lax.axis_index("dp"), lax.axis_index("mp")
    order_dp = me_dp ^ jnp.arange(dp, dtype=jnp.int32)
    steps, slots = session_ends.shape
    events = steps * slots
    feats, vocab = embedding.shape
    units = hid_weight.shape[2]
    width = up(units, 128)
    full = mp * width
    neg_count = negatives.shape[0]
    neg_share = neg_count // dp

    end_float = session_ends.astype(F32)
    keep = jnp.concatenate([jnp.zeros((1, slots), F32), 1.0 - end_float[:-1]], axis=0)
    weight = ((1.0 - end_float) / (steps * slots * dp)).reshape(events, 1)
    sources = item_ids[:-1].reshape(events)
    targets = item_ids[1:].reshape(events)
    own_negs = lax.dynamic_slice_in_dim(negatives, me_dp * neg_share, neg_share)

    def padded_rows(value):
        value = value.reshape(3, mp, units, units)
        value = jnp.pad(value, ((0, 0), (0, 0), (0, width - units), (0, width - units)))
        return value.reshape(3 * full, width)

    share = 3 * full // dp
    in_share = lax.dynamic_slice_in_dim(padded_rows(in_weight), me_dp * share, share)
    hid_share = lax.dynamic_slice_in_dim(padded_rows(hid_weight), me_dp * share, share)
    biases = jnp.pad(
        jnp.concatenate([gate_bias, cand_bias[None]]), ((0, 0), (0, width - units))
    )
    first = low(biases)
    second = low(biases - first.astype(F32))
    third = low(biases - first.astype(F32) - second.astype(F32))
    bias_rows = jnp.concatenate([first, second, third, jnp.zeros((4, width), BF)])
    in_cols = gather_mp(jnp.concatenate([in_share, bias_rows]))
    bias_all = in_cols[share : share + 12].astype(F32)
    bias_all = bias_all[0:4] + bias_all[4:8] + bias_all[8:12]
    in_full = place(gather_dp(in_cols[:share]), order_dp, 0).reshape(3, full, full)
    hid_cols = gather_mp(hid_share)
    hid_full = place(gather_dp(hid_cols), order_dp, 0).reshape(3, full, full)

    x_rows = lookup(sources, embedding)[:events]
    x_all = gather_mp(x_rows)
    t_rows = lookup(jnp.concatenate([targets, own_negs]), out_table, out_bias)
    t_all = gather_mp(t_rows[: events + neg_share])
    tgt = t_all[:events]
    neg = jnp.concatenate(gather_dp(t_all[events:]))

    gi = jnp.einsum("ne,geh->gnh", x_all, in_full, preferred_element_type=F32)
    gi = gi.reshape(3, steps, slots, full)
    saved = []
    hidden = None
    for t in range(steps):
        if t == 0:
            prev = jnp.zeros((slots, full), F32)
            low_prev = low(prev)
            update = jax.nn.sigmoid(gi[0, t] + bias_all[0])
            reset = jax.nn.sigmoid(gi[1, t] + bias_all[1])
            inner = jnp.broadcast_to(bias_all[3], (slots, full))
        else:
            prev = hidden * keep[t][:, None]
            low_prev = low(prev)
            gh = jnp.einsum("bk,gkh->gbh", low_prev, hid_full, preferred_element_type=F32)
            update = jax.nn.sigmoid(gi[0, t] + gh[0] + bias_all[0])
            reset = jax.nn.sigmoid(gi[1, t] + gh[1] + bias_all[1])
            inner = gh[2] + bias_all[3]
        cand = jnp.tanh(gi[2, t] + bias_all[2] + reset * inner)
        hidden = (1.0 - update) * prev + update * cand
        saved.append((prev, low_prev, update, reset, inner, cand, hidden))
    shown = low(jnp.concatenate([s[6] for s in saved]))

    col = jnp.arange(full)
    is_bias = (col >= units) & (col < units + 3)
    shown_one = jnp.where(is_bias[None, :], BF(1.0), shown)
    s = jnp.einsum("nh,jh->nj", shown_one, neg, preferred_element_type=F32)
    u = jnp.sum(shown_one.astype(F32) * tgt.astype(F32), axis=1, keepdims=True)
    prob = jax.nn.softmax(s, axis=1)
    above = jax.nn.sigmoid(u - s)
    mixture = jnp.sum(prob * above, axis=1, keepdims=True)
    spread = jnp.sum(prob * s * s, axis=1, keepdims=True)
    loss_part = jnp.sum(weight * (-jnp.log(mixture) + bpr_weight * spread))
    neg_grad = weight * prob * (
        1.0 - above * above / mixture + bpr_weight * (s * s + 2.0 * s - spread)
    )
    tgt_grad = -weight * jnp.sum(prob * above * (1.0 - above), axis=1, keepdims=True) / mixture
    neg_low = low(neg_grad)
    tgt_low = low(tgt_grad)
    dhs = jnp.dot(neg_low, neg, preferred_element_type=F32) + tgt_low.astype(F32) * tgt.astype(F32)
    dhs = dhs.reshape(steps, slots, full)

    own_cols = lambda v: lax.dynamic_slice_in_dim(v, me_mp * width, width, axis=v.ndim - 1)
    own_shown = own_cols(shown)
    spare = jnp.arange(width)[None, :]
    tgt_hi = (targets // 256).astype(BF)[:, None]
    tgt_lo = (targets % 256).astype(BF)[:, None]
    rows = jnp.where(
        spare == units,
        tgt_low,
        jnp.where(spare == units + 1, tgt_hi, jnp.where(spare == units + 2, tgt_lo, own_shown)),
    )
    rows_all = gather_dp(rows)
    counted = jnp.where(spare == units, BF(1.0), own_shown)
    neg_table = jnp.einsum("nj,nh->jh", neg_low, counted, preferred_element_type=F32)
    neg_sum = reduce_dp([neg_table[k * neg_share : (k + 1) * neg_share] for k in range(dp)])
    neg_sum = jnp.where(spare == units + 1, own_negs.astype(F32)[:, None], neg_sum)
    neg_all = gather_dp(neg_sum)

    in_own = lax.dynamic_slice_in_dim(in_full, me_mp * width, width, axis=1)
    later = jnp.zeros((slots, full), F32)
    bias_sums = 0.0
    gi_low, gh_low, dx_all = [None] * steps, [None] * steps, []
    for t in reversed(range(steps)):
        prev, low_prev, update, reset, inner, cand, _ = saved[t]
        dh = later + dhs[t]
        dz = dh * (cand - prev) * update * (1.0 - update)
        da = dh * update * (1.0 - cand * cand)
        dr = da * inner * reset * (1.0 - reset)
        dq = da * reset
        zl, rl, al, ql = low(dz), low(dr), low(da), low(dq)
        bias_sums = bias_sums + jnp.stack([jnp.sum(own_cols(v), axis=0) for v in (dz, dr, da, dq)])
        if t > 0:
            back = jnp.einsum(
                "gbh,gkh->bk", jnp.stack([zl, rl, ql]), hid_full, preferred_element_type=F32
            )
            later = (dh * (1.0 - update) + back) * keep[t][:, None]
        dx = jnp.einsum("gbh,gkh->bk", jnp.stack([zl, rl, al]), in_own, preferred_element_type=F32)
        dx = jnp.where(
            spare == units + 1, sources[t * slots : (t + 1) * slots].astype(F32)[:, None], dx
        )
        dx_all += gather_dp(dx)
        gi_low[t] = jnp.stack([own_cols(v) for v in (zl, rl, al)])
        gh_low[t] = jnp.stack([own_cols(v) for v in (zl, rl, ql)])

    def summed(parts):
        flat = parts.reshape(dp, share, width)
        blocks = [lax.dynamic_index_in_dim(flat, order_dp[k], 0, keepdims=False) for k in range(dp)]
        return place(gather_dp(reduce_dp(blocks)), order_dp, 0).reshape(3, mp, width, width)

    low_prevs = jnp.concatenate([saved[t][1] for t in range(1, steps)])
    hid_parts = jnp.einsum(
        "nk,gnh->gkh", low_prevs, jnp.concatenate(gh_low[1:], axis=1), preferred_element_type=F32
    )
    hid_sum = summed(hid_parts)
    in_parts = jnp.einsum(
        "ne,gnh->geh", x_all, jnp.concatenate(gi_low, axis=1), preferred_element_type=F32
    )
    in_parts = in_parts.at[0, units : units + 2].set(bias_sums[0:2])
    in_parts = in_parts.at[1, units : units + 2].set(bias_sums[2:4])
    in_parts = in_parts.at[2, units].set(jnp.full((width,), loss_part))
    in_sum = summed(in_parts)

    gate_sum = jnp.stack([in_sum[0, 0, units], in_sum[0, 0, units + 1], in_sum[1, 0, units]])
    gate_sum, cand_sum = gate_sum[:, :units], in_sum[1, 0, units + 1, :units]
    loss_value = in_sum[2, 0, units, 0]
    unpad = lambda v: v[:, :, :units, :units].reshape(3, mp * units, units)

    items = vocab // dp
    base = (me_dp * items).astype(jnp.int32).reshape(1)
    table_sum = scatter(
        base,
        units,
        items,
        [jnp.stack(rows_all).reshape(-1, slots, width), jnp.stack(neg_all)],
        ("coded", "plain"),
    )
    embed_sum = scatter(base, units, items, [jnp.stack(dx_all)], ("plain",))
    return (
        loss_value,
        unpad(in_sum),
        unpad(hid_sum),
        gate_sum,
        cand_sum,
        embed_sum[:feats],
        table_sum[:units],
        table_sum[units],
    )


def solution(mesh):
    return jax.shard_map(
        on_device,
        mesh=mesh,
        in_specs=(
            P(None, "dp"),
            P(None, "dp"),
            P(),
            P("mp", None),
            P(None, None, "mp"),
            P(None, None, "mp"),
            P(None, "mp"),
            P("mp"),
            P("mp", None),
            P(),
        ),
        out_specs=(
            P(),
            P(None, None, "mp"),
            P(None, None, "mp"),
            P(None, "mp"),
            P("mp"),
            P("mp", "dp"),
            P("mp", "dp"),
            P("dp"),
        ),
        check_vma=False,
    )
```

```python
import functools

import jax
import jax.numpy as jnp
from jax import lax
from jax.experimental import pallas as pl
from jax.experimental.pallas import tpu as pltpu
from jax.sharding import PartitionSpec as P

bpr_weight = 1.0
BF = jnp.bfloat16
F32 = jnp.float32
ITEM_BLOCK = 4096
CHUNK = 256
MIB = 1024 * 1024


def up(count, unit):
    return -(-count // unit) * unit


def lookup_kernel(has_bias, feats, cnt_ref, idr_ref, idc_ref, tab_ref, *rest):
    if has_bias:
        bias_ref, out_ref, sid, order, perm, xs, held, sems = rest
    else:
        out_ref, sid, order, perm, xs, held, sems = rest
    count = idr_ref.shape[1]
    blocks, _, width = held.shape

    def fetch(b):
        return pltpu.make_async_copy(
            tab_ref.at[:, pl.ds(b * width, width)], held.at[b], sems.at[b]
        )

    for b in range(blocks):
        fetch(b).start()
    lane = lax.broadcasted_iota(jnp.int32, (CHUNK, count), 1)
    keyr = idr_ref[...] * 4096 + lax.broadcasted_iota(jnp.int32, (1, count), 1)
    sid[...] = jnp.zeros_like(sid)
    order[...] = jnp.zeros_like(order)

    def sort_rows(i, _):
        rows = pl.ds(pl.multiple_of(i * CHUNK, CHUNK), CHUNK)
        idc = idc_ref[rows, :]
        at = i * CHUNK + lax.broadcasted_iota(jnp.int32, (CHUNK, 1), 0)
        keyc = idc * 4096 + at
        rank = jnp.sum((keyr < keyc).astype(F32), axis=1, keepdims=True).astype(jnp.int32)
        hit = rank == lane
        perm[rows, :] = hit.astype(F32).astype(BF)
        sid[...] += jnp.sum(jnp.where(hit, idc, 0).astype(F32), axis=0, keepdims=True)
        order[...] += jnp.sum(jnp.where(hit, at, 0).astype(F32), axis=0, keepdims=True)
        return 0

    lax.fori_loop(0, count // CHUNK, sort_rows, 0)
    xs[...] = jnp.zeros_like(xs)
    for b in range(blocks):
        fetch(b).wait()
        base = b * width

        def pick_chunk(c, _, b=b, base=base):
            cols = pl.ds(pl.multiple_of(c * CHUNK, CHUNK), CHUNK)
            ids = sid[:, cols].astype(jnp.int32) - base
            pick = (lax.broadcasted_iota(jnp.int32, (width, CHUNK), 0) == ids).astype(F32).astype(BF)
            xs[0:feats, cols] += jnp.dot(held[b], pick, preferred_element_type=F32)
            if has_bias:
                low = feats // 8 * 8
                value = bias_ref[:, base : base + width]
                first = value.astype(BF).astype(F32)
                second = (value - first).astype(BF).astype(F32)
                third = value - first - second
                row = lax.broadcasted_iota(jnp.int32, (8, width), 0) - (feats - low)
                parts = jnp.where(
                    row == 0, first, jnp.where(row == 1, second, jnp.where(row == 2, third, 0.0))
                ).astype(BF)
                xs[low : low + 8, cols] += jnp.dot(parts, pick, preferred_element_type=F32)
            return 0

        lax.fori_loop(
            cnt_ref[b] // CHUNK, (cnt_ref[b + 1] + CHUNK - 1) // CHUNK, pick_chunk, 0
        )
    out_ref[...] = lax.dot_general(
        perm[...], xs[...].astype(BF), (((1,), (1,)), ((), ())), preferred_element_type=F32
    ).astype(BF)


def lookup(ids, table, bias=None):
    feats, vocab = table.shape
    width = up(feats, 128)
    count = ids.shape[0]
    padded = up(count, CHUNK)
    ids = jnp.concatenate([ids, jnp.full((padded - count,), vocab, jnp.int32)])
    blocks = vocab // ITEM_BLOCK
    edges = jnp.arange(blocks + 1, dtype=jnp.int32) * ITEM_BLOCK
    cnt = jnp.sum((ids[None, :] < edges[:, None]).astype(jnp.int32), axis=1)
    vmem = pl.BlockSpec(memory_space=pltpu.VMEM)
    in_specs = [pl.BlockSpec(memory_space=pltpu.SMEM), vmem, vmem, pl.BlockSpec(memory_space=pl.ANY)]
    args = [cnt, ids.reshape(1, padded), ids.reshape(padded, 1), table]
    if bias is not None:
        in_specs.append(vmem)
        args.append(bias.reshape(1, vocab))
    return pl.pallas_call(
        functools.partial(lookup_kernel, bias is not None, feats),
        in_specs=in_specs,
        out_specs=[vmem, vmem, vmem],
        scratch_shapes=[
            pltpu.VMEM((padded, padded), BF),
            pltpu.VMEM((width, padded), F32),
            pltpu.VMEM((blocks, feats, ITEM_BLOCK), BF),
            pltpu.SemaphoreType.DMA((blocks,)),
        ],
        out_shape=[
            jax.ShapeDtypeStruct((padded, width), BF),
            jax.ShapeDtypeStruct((1, padded), F32),
            jax.ShapeDtypeStruct((1, padded), F32),
        ],
        compiler_params=pltpu.CompilerParams(vmem_limit_bytes=56 * MIB),
        cost_estimate=pl.CostEstimate(
            flops=2 * vocab * feats * 512, bytes_accessed=vocab * feats * 2, transcendentals=0
        ),
    )(*args)


def scatter_kernel(feats, plan, base_ref, edge_ref, list_ref, *refs):
    refs = list(refs)
    scale_ref = refs.pop(0) if plan["scaled"] else None
    pieces = [refs.pop(0) for _ in range(plan["pieces"])]
    negs = [refs.pop(0) for _ in range(plan["negs"])]
    if plan["scaled"]:
        out_ref, bias_ref, total, held = refs
    else:
        out_ref, total = refs
    sources = plan["pieces"]
    base = base_ref[0]
    items, width = total.shape
    total[...] = jnp.zeros_like(total)
    if plan["scaled"]:
        depth = pieces[0].shape[0]
        each = held.shape[0] // sources
        col = lax.broadcasted_iota(jnp.int32, (depth, width), 1)
        for s in range(sources):
            wide = pieces[s][...].astype(F32)
            held[s * each : s * each + depth, :] = jnp.where(col == feats, 1.0, wide)
            held[s * each + depth : (s + 1) * each, :] = negs[s][...]

    for s in range(sources):

        def add(r, _, s=s):
            item = list_ref[s, 0, r] - base
            row = list_ref[s, 1, r]
            if plan["scaled"]:
                value = held[pl.ds(s * each + row, 1), :] * scale_ref[s, row]
            else:
                value = pieces[s][pl.ds(row, 1), :]
            total[pl.ds(item, 1), :] += value
            return 0

        lax.fori_loop(edge_ref[s, 0], edge_ref[s, 1], add, 0)
    tile = 512 if items % 512 == 0 else 128
    for at in range(0, items, tile):
        turned = total[at : at + tile, :].T
        out_ref[:, at : at + tile] = turned[:feats]
        if plan["scaled"]:
            bias_ref[:, at : at + tile] = turned[feats : feats + 1]


def scatter(base, feats, items, lists, pieces, scale=None, negs=()):
    width = pieces[0].shape[-1]
    sources = len(pieces)
    each = pieces[0].shape[0] + (negs[0].shape[0] if negs else 0)
    below = lambda v: jnp.sum((lists[:, 0] < v).astype(jnp.int32), axis=1)
    edges = jnp.stack([below(base), below(base + items)], axis=1)
    scaled = scale is not None
    plan = {"scaled": scaled, "pieces": sources, "negs": len(negs)}
    smem = pl.BlockSpec(memory_space=pltpu.SMEM)
    vmem = pl.BlockSpec(memory_space=pltpu.VMEM)
    out_shape = [jax.ShapeDtypeStruct((feats, items), F32)]
    scratch = [pltpu.VMEM((items, width), F32)]
    if scaled:
        out_shape.append(jax.ShapeDtypeStruct((1, items), F32))
        scratch.append(pltpu.VMEM((sources * each, width), F32))
    return pl.pallas_call(
        functools.partial(scatter_kernel, feats, plan),
        in_specs=[smem] * (4 if scaled else 3) + [vmem] * (sources + len(negs)),
        out_specs=[vmem] * len(out_shape),
        out_shape=out_shape,
        scratch_shapes=scratch,
        compiler_params=pltpu.CompilerParams(vmem_limit_bytes=56 * MIB),
        cost_estimate=pl.CostEstimate(
            flops=0, bytes_accessed=sources * each * width * 8, transcendentals=0
        ),
    )(base.reshape(1), edges, lists, *([scale] if scaled else []), *pieces, *negs)


def place_kernel(axis, where_ref, *refs):
    *pieces, out_ref, sems = refs
    copies = []
    for k, piece in enumerate(pieces):
        size = piece.shape[axis]
        spot = pl.ds(pl.multiple_of(where_ref[k] * size, size), size)
        target = out_ref.at[spot, :] if axis == 0 else out_ref.at[:, spot]
        copies.append(pltpu.make_async_copy(piece, target, sems.at[k]))
    for copy in copies:
        copy.start()
    for copy in copies:
        copy.wait()


def place(pieces, where, axis):
    shape = list(pieces[0].shape)
    shape[axis] *= len(pieces)
    anywhere = pl.BlockSpec(memory_space=pl.ANY)
    return pl.pallas_call(
        functools.partial(place_kernel, axis),
        in_specs=[pl.BlockSpec(memory_space=pltpu.SMEM)] + [anywhere] * len(pieces),
        out_specs=pl.BlockSpec(memory_space=pltpu.VMEM),
        scratch_shapes=[pltpu.SemaphoreType.DMA((len(pieces),))],
        out_shape=jax.ShapeDtypeStruct(tuple(shape), pieces[0].dtype),
        compiler_params=pltpu.CompilerParams(vmem_limit_bytes=32 * MIB),
        cost_estimate=pl.CostEstimate(
            flops=0, bytes_accessed=2 * sum(p.size * p.dtype.itemsize for p in pieces), transcendentals=0
        ),
    )(where, *pieces)


def forward_kernel(
    x_ref, keep_ref, in_ref, hid_ref, bias_ref, z_ref, r_ref, c_ref, q_ref, prev_ref, hb_ref, hs_ref, state, low_state
):
    t, q = pl.program_id(0), pl.program_id(1)
    width = z_ref.shape[2]
    cols = pl.ds(pl.multiple_of(q * width, width), width)

    @pl.when(t == 0)
    def _():
        state[:, cols] = jnp.zeros_like(prev_ref[0])

    @pl.when(q == 0)
    def _():
        low_state[...] = (state[...] * keep_ref[0]).astype(BF)

    x = x_ref[...]
    gi = [jnp.dot(x, in_ref[g], preferred_element_type=F32) + bias_ref[g : g + 1, :] for g in range(3)]
    q_ref[0] = jnp.broadcast_to(bias_ref[3:4, :], q_ref.shape[1:])
    z_ref[0] = gi[0]
    r_ref[0] = gi[1]

    @pl.when(t > 0)
    def _():
        low_prev = low_state[...]
        z_ref[0] += jnp.dot(low_prev, hid_ref[0], preferred_element_type=F32)
        r_ref[0] += jnp.dot(low_prev, hid_ref[1], preferred_element_type=F32)
        q_ref[0] += jnp.dot(low_prev, hid_ref[2], preferred_element_type=F32)

    prev = state[:, cols] * keep_ref[0]
    z = 1.0 / (1.0 + jnp.exp(-z_ref[0]))
    r = 1.0 / (1.0 + jnp.exp(-r_ref[0]))
    c = jnp.tanh(gi[2] + r * q_ref[0])
    h = (1.0 - z) * prev + z * c
    z_ref[0] = z
    r_ref[0] = r
    c_ref[0] = c
    prev_ref[0] = prev
    hb_ref[0] = prev.astype(BF)
    hs_ref[0] = h.astype(BF)
    state[:, cols] = h


def forward(steps, slots, width, x_all, keep, in_full, hid_full, bias_all):
    full = in_full.shape[2]
    parts = full // width
    tile = pl.BlockSpec((1, slots, width), lambda t, q: (t, 0, q))
    shape = lambda dtype: jax.ShapeDtypeStruct((steps, slots, full), dtype)
    return pl.pallas_call(
        forward_kernel,
        grid=(steps, parts),
        in_specs=[
            pl.BlockSpec((slots, full), lambda t, q: (t, 0)),
            pl.BlockSpec((1, slots, 1), lambda t, q: (t, 0, 0)),
            pl.BlockSpec((3, full, width), lambda t, q: (0, 0, q)),
            pl.BlockSpec((3, full, width), lambda t, q: (0, 0, jnp.where(t == 0, 0, q))),
            pl.BlockSpec((8, width), lambda t, q: (0, q)),
        ],
        out_specs=[tile] * 7,
        out_shape=[shape(F32)] * 5 + [shape(BF)] * 2,
        scratch_shapes=[pltpu.VMEM((slots, full), F32), pltpu.VMEM((slots, full), BF)],
        compiler_params=pltpu.CompilerParams(vmem_limit_bytes=48 * MIB),
        cost_estimate=pl.CostEstimate(
            flops=2 * 6 * steps * slots * full * full,
            bytes_accessed=steps * full * (slots * 24 + full * 12),
            transcendentals=3 * steps * slots * full,
        ),
    )(x_all, keep, in_full, hid_full, bias_all)


def score_kernel(
    rows, hs_ref, one_ref, tgt_ref, neg_ref, weight_ref, ds_ref, dhs_ref, du_ref, loss_ref, s_ref
):
    shown = hs_ref[...]
    s_ref[...] = lax.dot_general(
        shown + one_ref[...], neg_ref[...], (((1,), (1,)), ((), ())), preferred_element_type=F32
    )

    @pl.when(pl.program_id(0) == 0)
    def _():
        loss_ref[...] = jnp.zeros_like(loss_ref)

    def chunk(i, _):
        at = pl.ds(pl.multiple_of(i * rows, rows), rows)
        s = s_ref[at, :]
        w = weight_ref[at, :]
        tgt = tgt_ref[at, :].astype(F32)
        u = jnp.sum((hs_ref[at, :] + one_ref[...]).astype(F32) * tgt, axis=1, keepdims=True)
        top = jnp.max(s, axis=1, keepdims=True)
        e = jnp.exp(s - top)
        above = 1.0 / (1.0 + jnp.exp(s - u))
        ea = e * above
        inv = 1.0 / jnp.sum(e, axis=1, keepdims=True)
        mixture = jnp.sum(ea, axis=1, keepdims=True) * inv
        spread = jnp.sum(e * s * s, axis=1, keepdims=True) * inv
        slope = jnp.sum(ea * (1.0 - above), axis=1, keepdims=True) * inv
        ds = (w * inv) * e * (1.0 - above * above * (1.0 / mixture) + bpr_weight * (s * s + 2.0 * s - spread))
        ds_ref[at, :] = ds.astype(BF)
        du_ref[at, :] = (-w * slope / mixture).astype(BF).astype(F32)
        loss_ref[...] += jnp.broadcast_to(
            jnp.sum(w * (-jnp.log(mixture) + bpr_weight * spread), keepdims=True), loss_ref.shape
        )
        return 0

    lax.fori_loop(0, s_ref.shape[0] // rows, chunk, 0)
    dhs_ref[...] = (
        jnp.dot(ds_ref[...], neg_ref[...], preferred_element_type=F32)
        + du_ref[...] * tgt_ref[...].astype(F32)
    )


def scores(tile, shown, one_row, t_all, neg, weight):
    events, full = shown.shape
    count = neg.shape[0]
    row_tile = lambda w: pl.BlockSpec((tile, w), lambda i: (i, 0))
    return pl.pallas_call(
        functools.partial(score_kernel, 32),
        grid=(events // tile,),
        in_specs=[
            row_tile(full),
            pl.BlockSpec((1, full), lambda i: (0, 0)),
            row_tile(full),
            pl.BlockSpec(memory_space=pltpu.VMEM),
            row_tile(1),
        ],
        out_specs=[row_tile(count), row_tile(full), row_tile(1), pl.BlockSpec((8, 128), lambda i: (0, 0))],
        out_shape=[
            jax.ShapeDtypeStruct((events, count), BF),
            jax.ShapeDtypeStruct((events, full), F32),
            jax.ShapeDtypeStruct((events, 1), F32),
            jax.ShapeDtypeStruct((8, 128), F32),
        ],
        scratch_shapes=[pltpu.VMEM((tile, count), F32)],
        compiler_params=pltpu.CompilerParams(vmem_limit_bytes=48 * MIB),
        cost_estimate=pl.CostEstimate(
            flops=4 * events * full * count,
            bytes_accessed=events * (full * 8 + count * 2) + count * full * 2,
            transcendentals=3 * events * count,
        ),
    )(shown, one_row, t_all, neg, weight)


def backward_kernel(
    me_ref, z_ref, r_ref, c_ref, q_ref, prev_ref, keep_ref, dhs_ref, hid_ref, in_ref, dx_ref, own_ref, sum_ref, later, back
):
    i, q = pl.program_id(0), pl.program_id(1)
    last_step, last_part = pl.num_programs(0) - 1, pl.num_programs(1) - 1
    width = z_ref.shape[2]
    cols = pl.ds(pl.multiple_of(q * width, width), width)

    @pl.when((i == 0) & (q == 0))
    def _():
        later[...] = jnp.zeros_like(later)
        sum_ref[...] = jnp.zeros_like(sum_ref)

    @pl.when(q == 0)
    def _():
        dx_ref[...] = jnp.zeros_like(dx_ref)
        back[...] = jnp.zeros_like(back)

    z, r, c, inner = z_ref[0], r_ref[0], c_ref[0], q_ref[0]
    dh = later[:, cols] + dhs_ref[...]
    dz = dh * (c - prev_ref[0]) * z * (1.0 - z)
    da = dh * z * (1.0 - c * c)
    dr = da * inner * r * (1.0 - r)
    dq = da * r
    grads = (dz, dr, da, dq)
    zl, rl, al, ql = [v.astype(BF) for v in grads]
    over = (((1,), (1,)), ((), ()))
    for value, g in ((zl, 0), (rl, 1), (al, 2)):
        dx_ref[...] += lax.dot_general(value, in_ref[g], over, preferred_element_type=F32)

    @pl.when(i < last_step)
    def _():
        total = lax.dot_general(zl, hid_ref[0], over, preferred_element_type=F32)
        total += lax.dot_general(rl, hid_ref[1], over, preferred_element_type=F32)
        total += lax.dot_general(ql, hid_ref[2], over, preferred_element_type=F32)
        back[...] += total
        back[:, cols] += dh * (1.0 - z)

    @pl.when(q == me_ref[0])
    def _():
        for k, value in enumerate((zl, rl, al, ql)):
            own_ref[:, k * width : (k + 1) * width] = value
            sum_ref[k : k + 1, :] += jnp.sum(grads[k], axis=0, keepdims=True)

    @pl.when(q == last_part)
    def _():
        later[...] = back[...] * keep_ref[0]


def backward(width, me, z, r, c, inner, prev, keep, dhs, hid_full, in_full):
    steps, slots, full = z.shape
    parts = full // width
    tile = pl.BlockSpec((1, slots, width), lambda i, q, me: (steps - 1 - i, 0, q))
    row = lambda w: pl.BlockSpec((slots, w), lambda i, q, me: (steps - 1 - i, 0))
    return pl.pallas_call(
        backward_kernel,
        grid_spec=pltpu.PrefetchScalarGridSpec(
            num_scalar_prefetch=1,
            grid=(steps, parts),
            in_specs=[tile] * 5
            + [
                pl.BlockSpec((1, slots, 1), lambda i, q, me: (steps - 1 - i, 0, 0)),
                pl.BlockSpec((slots, width), lambda i, q, me: (steps - 1 - i, q)),
                pl.BlockSpec((3, full, width), lambda i, q, me: (0, 0, jnp.where(i == steps - 1, parts - 1, q))),
                pl.BlockSpec((3, width, width), lambda i, q, me: (0, me[0], q)),
            ],
            out_specs=[row(width), row(4 * width), pl.BlockSpec((8, width), lambda i, q, me: (0, 0))],
            scratch_shapes=[pltpu.VMEM((slots, full), F32), pltpu.VMEM((slots, full), F32)],
        ),
        out_shape=[
            jax.ShapeDtypeStruct((steps * slots, width), F32),
            jax.ShapeDtypeStruct((steps * slots, 4 * width), BF),
            jax.ShapeDtypeStruct((8, width), F32),
        ],
        compiler_params=pltpu.CompilerParams(vmem_limit_bytes=48 * MIB),
        cost_estimate=pl.CostEstimate(
            flops=2 * steps * slots * full * (3 * full + 3 * width),
            bytes_accessed=steps * full * (slots * 24 + full * 6),
            transcendentals=0,
        ),
    )(me, z, r, c, inner, prev, keep, dhs, hid_full, in_full)


def weights_kernel(units, order_ref, x_ref, hb_ref, own_ref, sum_ref, loss_ref, kept_ref, sent_ref, total):
    width = sum_ref.shape[1]
    slots = x_ref.shape[0] - hb_ref.shape[0]
    over = (((0,), (0,)), ((), ()))
    three = 3 * width
    total[:, :three] = lax.dot_general(x_ref[...], own_ref[:, :three], over, preferred_element_type=F32)
    hb = hb_ref[...]
    total[:, three : three + 2 * width] = lax.dot_general(
        hb, own_ref[slots:, : 2 * width], over, preferred_element_type=F32
    )
    total[:, three + 2 * width :] = lax.dot_general(
        hb, own_ref[slots:, three:], over, preferred_element_type=F32
    )
    for k in range(3):
        total[units : units + 1, k * width : (k + 1) * width] = sum_ref[k : k + 1, :]
    total[units + 1 : units + 2, :width] = sum_ref[3:4, :]
    total[units + 1 : units + 2, width : width + 128] = loss_ref[0:1, :]
    rows = kept_ref.shape[1]
    for k in range(kept_ref.shape[0]):
        for ref, at in ((kept_ref, 2 * k), (sent_ref, 2 * k + 1)):
            ref[k] = total[pl.ds(pl.multiple_of(order_ref[at] * rows, rows), rows), :]


def weight_grads(units, order, x_all, hb, own, sums, loss):
    full = x_all.shape[1]
    width = sums.shape[1]
    count = order.shape[0]
    half = jax.ShapeDtypeStruct((count // 2, full // count, 6 * width), F32)
    vmem = pl.BlockSpec(memory_space=pltpu.VMEM)
    return pl.pallas_call(
        functools.partial(weights_kernel, units),
        in_specs=[pl.BlockSpec(memory_space=pltpu.SMEM)] + [vmem] * 5,
        out_specs=[vmem, vmem],
        out_shape=[half, half],
        scratch_shapes=[pltpu.VMEM((full, 6 * width), F32)],
        compiler_params=pltpu.CompilerParams(vmem_limit_bytes=56 * MIB),
        cost_estimate=pl.CostEstimate(
            flops=2 * x_all.shape[0] * full * 6 * width,
            bytes_accessed=x_all.size * 4 + full * 24 * width,
            transcendentals=0,
        ),
    )(order, x_all, hb, own, sums, loss)


def swap(value, k, axis):
    count = lax.axis_size(axis)
    return lax.ppermute(value, axis, [(i, i ^ k) for i in range(count)])


def gather_mp(value):
    count = lax.axis_size("mp")
    pieces = [value] + [swap(value, k, "mp") for k in range(1, count)]
    where = lax.axis_index("mp") ^ jnp.arange(count, dtype=jnp.int32)
    return place(pieces, where, 1)


def gather_dp(value):
    count = lax.axis_size("dp")
    chips = [value] + [swap(value, k, "dp") for k in range(2, count, 2)]
    other = [swap(piece, 1, "dp") for piece in chips]
    return [piece for pair in zip(chips, other) for piece in pair]


def reduce_dp(kept, sent):
    mine = kept + swap(sent, 1, "dp")
    total = mine[0]
    for k in range(1, mine.shape[0]):
        total = total + swap(mine[k], 2 * k, "dp")
    return total


def low(value):
    return lax.reduce_precision(value, 8, 7).astype(BF)


def on_device(
    item_ids,
    session_ends,
    negatives,
    embedding,
    in_weight,
    hid_weight,
    gate_bias,
    cand_bias,
    out_table,
    out_bias,
):
    dp, mp = lax.axis_size("dp"), lax.axis_size("mp")
    me_dp, me_mp = lax.axis_index("dp"), lax.axis_index("mp")
    order_dp = me_dp ^ jnp.arange(dp, dtype=jnp.int32)
    steps, slots = session_ends.shape
    events = steps * slots
    feats, vocab = embedding.shape
    units = hid_weight.shape[2]
    width = up(units, 128)
    full = mp * width
    neg_count = negatives.shape[0]
    neg_share = neg_count // dp

    end_float = session_ends.astype(F32)
    keep = jnp.concatenate([jnp.zeros((1, slots), F32), 1.0 - end_float[:-1]], axis=0)
    weight = ((1.0 - end_float) / (steps * slots * dp)).reshape(events, 1)
    sources = item_ids[:-1].reshape(events)
    targets = item_ids[1:].reshape(events)
    own_negs = lax.dynamic_slice_in_dim(negatives, me_dp * neg_share, neg_share)

    def padded_rows(value):
        value = value.reshape(3, mp, units, units)
        value = jnp.pad(value, ((0, 0), (0, 0), (0, width - units), (0, width - units)))
        return value.reshape(3 * full, width)

    share = 3 * full // dp
    in_share = lax.dynamic_slice_in_dim(padded_rows(in_weight), me_dp * share, share)
    hid_share = lax.dynamic_slice_in_dim(padded_rows(hid_weight), me_dp * share, share)
    biases = jnp.pad(
        jnp.concatenate([gate_bias, cand_bias[None]]), ((0, 0), (0, width - units))
    )
    first = low(biases)
    second = low(biases - first.astype(F32))
    third = low(biases - first.astype(F32) - second.astype(F32))
    bias_rows = jnp.concatenate([first, second, third, jnp.zeros((4, width), BF)])
    in_cols = gather_mp(jnp.concatenate([in_share, bias_rows]))
    bias_all = in_cols[share : share + 12].astype(F32)
    bias_all = jnp.pad(bias_all[0:4] + bias_all[4:8] + bias_all[8:12], ((0, 4), (0, 0)))
    in_full = place(gather_dp(in_cols[:share]), order_dp, 0).reshape(3, full, full)
    hid_cols = gather_mp(hid_share)
    hid_full = place(gather_dp(hid_cols), order_dp, 0).reshape(3, full, full)

    x_rows, x_sid, x_order = lookup(sources, embedding)
    x_all = gather_mp(x_rows[:events])
    t_rows, t_sid, t_order = lookup(jnp.concatenate([targets, own_negs]), out_table, out_bias)
    t_all = gather_mp(t_rows[: events + neg_share])
    neg = jnp.concatenate(gather_dp(t_all[events:]))
    gap = ((0, 0), (0, t_sid.shape[1] - x_sid.shape[1]))
    lists = jnp.concatenate([jnp.pad(x_sid, gap), jnp.pad(x_order, gap), t_sid, t_order])
    lists = jnp.stack(gather_dp(lists.astype(jnp.int32)))
    x_lists = lists[:, 0:2, : x_sid.shape[1]]
    t_lists = lists[:, 2:4]

    z, r, c, inner, prev, hb, hs = forward(
        steps, slots, width, x_all, keep[:, :, None], in_full, hid_full, bias_all
    )
    shown = hs.reshape(events, full)
    col = jnp.arange(full)[None, :]
    one_row = ((col >= units) & (col < units + 3)).astype(BF)
    own_shown = lax.dynamic_slice_in_dim(shown, me_mp * width, width, axis=1)
    rows_all = gather_dp(own_shown)

    neg_low, dhs, tgt_low, loss = scores(slots, shown, one_row, t_all, neg, weight)

    counted = jnp.where(jnp.arange(width)[None, :] == units, BF(1.0), own_shown)
    neg_table = jnp.einsum("nj,nh->jh", neg_low, counted, preferred_element_type=F32)
    neg_table = neg_table.reshape(dp // 2, 2, neg_share, width)
    neg_sum = reduce_dp(neg_table[:, 0], neg_table[:, 1])
    scale_rows = up(-(-events // width), 8)
    scale = jnp.pad(tgt_low.reshape(events), (0, scale_rows * width - events))
    neg_all = gather_dp(jnp.concatenate([neg_sum, scale.reshape(scale_rows, width)]))
    scale_all = jnp.stack([v[neg_share:].reshape(-1)[:events] for v in neg_all])
    scale_all = jnp.concatenate([scale_all, jnp.ones((dp, neg_share), F32)], axis=1)

    dx, own, sums = backward(
        width, me_mp.reshape(1), z, r, c, inner, prev, keep[:, :, None], dhs, hid_full, in_full
    )
    dx_all = gather_dp(dx)
    kept, sent = weight_grads(
        units, order_dp, x_all, hb.reshape(events, full)[slots:], own, sums, loss
    )
    grads = place(gather_dp(reduce_dp(kept, sent)), order_dp, 0)
    gate_sum = grads[units, : 3 * width].reshape(3, width)[:, :units]
    cand_sum = grads[units + 1, :units]
    loss_value = grads[units + 1, width]
    grads = grads.reshape(mp, width, 2, 3, width)[:, :units, :, :, :units]
    grads = grads.transpose(2, 3, 0, 1, 4).reshape(2, 3, mp * units, units)

    items = vocab // dp
    base = (me_dp * items).astype(jnp.int32)
    table_sum, bias_sum = scatter(
        base, units, items, t_lists, rows_all, scale_all, [v[:neg_share] for v in neg_all]
    )
    (embed_sum,) = scatter(base, units, items, x_lists, dx_all)
    return (
        loss_value,
        grads[0],
        grads[1],
        gate_sum,
        cand_sum,
        embed_sum,
        table_sum,
        bias_sum.reshape(items),
    )


def solution(mesh):
    return jax.shard_map(
        on_device,
        mesh=mesh,
        in_specs=(
            P(None, "dp"),
            P(None, "dp"),
            P(),
            P("mp", None),
            P(None, None, "mp"),
            P(None, None, "mp"),
            P(None, "mp"),
            P("mp"),
            P("mp", None),
            P(),
        ),
        out_specs=(
            P(),
            P(None, None, "mp"),
            P(None, None, "mp"),
            P(None, "mp"),
            P("mp"),
            P("mp", "dp"),
            P("mp", "dp"),
            P("dp"),
        ),
        check_vma=False,
    )
```

```python
import functools

import jax
import jax.numpy as jnp
from jax import lax
from jax.experimental import pallas as pl
from jax.experimental.pallas import tpu as pltpu
from jax.sharding import PartitionSpec as P

bpr_weight = 1.0
BF = jnp.bfloat16
F32 = jnp.float32
ITEM_BLOCK = 4096
CHUNK = 256
MIB = 1024 * 1024


def up(count, unit):
    return -(-count // unit) * unit


def lookup_kernel(has_bias, feats, cnt_ref, idr_ref, idc_ref, tab_ref, *rest):
    if has_bias:
        bias_ref, out_ref, sid, order, perm, xs, held, sems = rest
    else:
        out_ref, sid, order, perm, xs, held, sems = rest
    count = idr_ref.shape[1]
    blocks, _, width = held.shape

    def fetch(b):
        return pltpu.make_async_copy(
            tab_ref.at[:, pl.ds(b * width, width)], held.at[b], sems.at[b]
        )

    for b in range(blocks):
        fetch(b).start()
    lane = lax.broadcasted_iota(jnp.int32, (CHUNK, count), 1)
    keyr = idr_ref[...] * 4096 + lax.broadcasted_iota(jnp.int32, (1, count), 1)
    sid[...] = jnp.zeros_like(sid)
    order[...] = jnp.zeros_like(order)

    def sort_rows(i, _):
        rows = pl.ds(pl.multiple_of(i * CHUNK, CHUNK), CHUNK)
        idc = idc_ref[rows, :]
        at = i * CHUNK + lax.broadcasted_iota(jnp.int32, (CHUNK, 1), 0)
        keyc = idc * 4096 + at
        rank = jnp.sum((keyr < keyc).astype(F32), axis=1, keepdims=True).astype(jnp.int32)
        hit = rank == lane
        perm[rows, :] = hit.astype(F32).astype(BF)
        sid[...] += jnp.sum(jnp.where(hit, idc, 0).astype(F32), axis=0, keepdims=True)
        order[...] += jnp.sum(jnp.where(hit, at, 0).astype(F32), axis=0, keepdims=True)
        return 0

    lax.fori_loop(0, count // CHUNK, sort_rows, 0)
    xs[...] = jnp.zeros_like(xs)
    for b in range(blocks):
        fetch(b).wait()
        base = b * width

        def pick_chunk(c, _, b=b, base=base):
            cols = pl.ds(pl.multiple_of(c * CHUNK, CHUNK), CHUNK)
            ids = sid[:, cols].astype(jnp.int32) - base
            pick = (lax.broadcasted_iota(jnp.int32, (width, CHUNK), 0) == ids).astype(F32).astype(BF)
            xs[0:feats, cols] += jnp.dot(held[b], pick, preferred_element_type=F32)
            return 0

        lax.fori_loop(
            cnt_ref[b] // CHUNK, (cnt_ref[b + 1] + CHUNK - 1) // CHUNK, pick_chunk, 0
        )
    out = lax.dot_general(
        perm[...], xs[...].astype(BF), (((1,), (1,)), ((), ())), preferred_element_type=F32
    )
    if has_bias:
        value = bias_ref[...]
        first = value.astype(BF).astype(F32)
        second = (value - first).astype(BF).astype(F32)
        parts = (first, second, value - first - second)
        groups = value.shape[0]
        idc = idc_ref[...]
        group = (idc // 128 == lax.broadcasted_iota(jnp.int32, (count, groups), 1)).astype(F32).astype(BF)
        member = lax.broadcasted_iota(jnp.int32, (count, 128), 1) == idc % 128
        col = lax.broadcasted_iota(jnp.int32, out.shape, 1)
        for k, part in enumerate(parts):
            near = jnp.dot(group, part.astype(BF), preferred_element_type=F32)
            own = jnp.sum(jnp.where(member, near, 0.0), axis=1, keepdims=True)
            out = jnp.where(col == feats + k, own, out)
    out_ref[...] = out.astype(BF)


def lookup(ids, table, bias=None):
    feats, vocab = table.shape
    width = up(feats, 128)
    count = ids.shape[0]
    padded = up(count, CHUNK)
    ids = jnp.concatenate([ids, jnp.full((padded - count,), vocab, jnp.int32)])
    blocks = vocab // ITEM_BLOCK
    edges = jnp.arange(blocks + 1, dtype=jnp.int32) * ITEM_BLOCK
    cnt = jnp.sum((ids[None, :] < edges[:, None]).astype(jnp.int32), axis=1)
    vmem = pl.BlockSpec(memory_space=pltpu.VMEM)
    in_specs = [pl.BlockSpec(memory_space=pltpu.SMEM), vmem, vmem, pl.BlockSpec(memory_space=pl.ANY)]
    args = [cnt, ids.reshape(1, padded), ids.reshape(padded, 1), table]
    if bias is not None:
        in_specs.append(vmem)
        args.append(bias.reshape(vocab // 128, 128))
    return pl.pallas_call(
        functools.partial(lookup_kernel, bias is not None, feats),
        in_specs=in_specs,
        out_specs=[vmem, vmem, vmem],
        scratch_shapes=[
            pltpu.VMEM((padded, padded), BF),
            pltpu.VMEM((width, padded), F32),
            pltpu.VMEM((blocks, feats, ITEM_BLOCK), BF),
            pltpu.SemaphoreType.DMA((blocks,)),
        ],
        out_shape=[
            jax.ShapeDtypeStruct((padded, width), BF),
            jax.ShapeDtypeStruct((1, padded), F32),
            jax.ShapeDtypeStruct((1, padded), F32),
        ],
        compiler_params=pltpu.CompilerParams(vmem_limit_bytes=56 * MIB),
        cost_estimate=pl.CostEstimate(
            flops=2 * vocab * feats * 512, bytes_accessed=vocab * feats * 2, transcendentals=0
        ),
    )(*args)


def scatter_kernel(feats, plan, base_ref, edge_ref, list_ref, *refs):
    refs = list(refs)
    scale_ref = refs.pop(0) if plan["scaled"] else None
    pieces = [refs.pop(0) for _ in range(plan["pieces"])]
    negs = [refs.pop(0) for _ in range(plan["negs"])]
    if plan["scaled"]:
        out_ref, bias_ref, total, held = refs
    else:
        out_ref, total = refs
    sources = plan["pieces"]
    base = base_ref[0]
    items, width = total.shape
    total[...] = jnp.zeros_like(total)
    if plan["scaled"]:
        depth = pieces[0].shape[0]
        each = held.shape[0] // sources
        col = lax.broadcasted_iota(jnp.int32, (depth, width), 1)
        for s in range(sources):
            wide = pieces[s][...].astype(F32)
            held[s * each : s * each + depth, :] = jnp.where(col == feats, 1.0, wide)
            held[s * each + depth : (s + 1) * each, :] = negs[s][...]

    def term(s, r):
        row = list_ref[s, 1, r]
        if plan["scaled"]:
            return held[pl.ds(s * each + row, 1), :] * scale_ref[s, row]
        return pieces[s][pl.ds(row, 1), :]

    for s in range(sources):
        first, last = edge_ref[s, 0], edge_ref[s, 1]

        @pl.when(last > first)
        def _(s=s, first=first, last=last):
            item = list_ref[s, 0, first] - base
            value = total[pl.ds(item, 1), :] + term(s, first)

            def add(r, carry):
                item, value = carry
                new = list_ref[s, 0, r] - base
                ahead = total[pl.ds(new, 1), :]
                total[pl.ds(item, 1), :] = value
                return new, jnp.where(new == item, value, ahead) + term(s, r)

            item, value = lax.fori_loop(first + 1, last, add, (item, value))
            total[pl.ds(item, 1), :] = value

    tile = 512 if items % 512 == 0 else 128
    for at in range(0, items, tile):
        turned = total[at : at + tile, :].T
        out_ref[:, at : at + tile] = turned[:feats]
        if plan["scaled"]:
            bias_ref[:, at : at + tile] = turned[feats : feats + 1]


def scatter(base, feats, items, lists, pieces, scale=None, negs=()):
    width = pieces[0].shape[-1]
    sources = len(pieces)
    each = pieces[0].shape[0] + (negs[0].shape[0] if negs else 0)
    below = lambda v: jnp.sum((lists[:, 0] < v).astype(jnp.int32), axis=1)
    edges = jnp.stack([below(base), below(base + items)], axis=1)
    scaled = scale is not None
    plan = {"scaled": scaled, "pieces": sources, "negs": len(negs)}
    smem = pl.BlockSpec(memory_space=pltpu.SMEM)
    vmem = pl.BlockSpec(memory_space=pltpu.VMEM)
    out_shape = [jax.ShapeDtypeStruct((feats, items), F32)]
    scratch = [pltpu.VMEM((items, width), F32)]
    if scaled:
        out_shape.append(jax.ShapeDtypeStruct((1, items), F32))
        scratch.append(pltpu.VMEM((sources * each, width), F32))
    return pl.pallas_call(
        functools.partial(scatter_kernel, feats, plan),
        in_specs=[smem] * (4 if scaled else 3) + [vmem] * (sources + len(negs)),
        out_specs=[vmem] * len(out_shape),
        out_shape=out_shape,
        scratch_shapes=scratch,
        compiler_params=pltpu.CompilerParams(vmem_limit_bytes=56 * MIB),
        cost_estimate=pl.CostEstimate(
            flops=0, bytes_accessed=sources * each * width * 8, transcendentals=0
        ),
    )(base.reshape(1), edges, lists, *([scale] if scaled else []), *pieces, *negs)


def place_kernel(first, axis, where_ref, *refs):
    *pieces, out_ref, sems = refs
    size = out_ref.shape[axis] // len(pieces)
    copies = []
    for k, piece in enumerate(pieces):
        spot = pl.ds(pl.multiple_of(where_ref[k] * size, size), size)
        target = out_ref.at[spot, :] if axis == 0 else out_ref.at[:, spot]
        source = piece.at[pl.ds(first, target.shape[0]), :]
        copies.append(pltpu.make_async_copy(source, target, sems.at[k]))
    for copy in copies:
        copy.start()
    for copy in copies:
        copy.wait()


def place(pieces, where, axis, first=0, rows=None):
    shape = [rows or pieces[0].shape[0], pieces[0].shape[1]]
    shape[axis] *= len(pieces)
    anywhere = pl.BlockSpec(memory_space=pl.ANY)
    return pl.pallas_call(
        functools.partial(place_kernel, first, axis),
        in_specs=[pl.BlockSpec(memory_space=pltpu.SMEM)] + [anywhere] * len(pieces),
        out_specs=pl.BlockSpec(memory_space=pltpu.VMEM),
        scratch_shapes=[pltpu.SemaphoreType.DMA((len(pieces),))],
        out_shape=jax.ShapeDtypeStruct(tuple(shape), pieces[0].dtype),
        compiler_params=pltpu.CompilerParams(vmem_limit_bytes=16 * MIB),
        cost_estimate=pl.CostEstimate(
            flops=0, bytes_accessed=4 * shape[0] * shape[1], transcendentals=0
        ),
    )(where, *pieces)


def row_copies(pieces, where_ref, target, sems, first_sem):
    copies = []
    for k, piece in enumerate(pieces):
        size = piece.shape[0]
        at = pl.multiple_of(where_ref[k] * size, size) if where_ref is not None else k * size
        copies.append(
            pltpu.make_async_copy(piece, target.at[pl.ds(at, size), :], sems.at[first_sem + k])
        )
    return copies


def col_copies(pieces, where_ref, target, sems, first_sem):
    rows = target.shape[0]
    copies = []
    for k, piece in enumerate(pieces):
        size = piece.shape[1]
        spot = pl.ds(pl.multiple_of(where_ref[k] * size, size), size)
        copies.append(
            pltpu.make_async_copy(piece.at[pl.ds(0, rows), :], target.at[:, spot], sems.at[first_sem + k])
        )
    return copies


def start(copies):
    for copy in copies:
        copy.start()


def finish(copies):
    for copy in copies:
        copy.wait()


ANYWHERE = pl.BlockSpec(memory_space=pl.ANY)
IN_SMEM = pl.BlockSpec(memory_space=pltpu.SMEM)
IN_VMEM = pl.BlockSpec(memory_space=pltpu.VMEM)


def forward_kernel(mp, dp, me_ref, where_mp, where_dp, keep_ref, bias_ref, *refs):
    x_pieces, in_pieces, hid_pieces = refs[:mp], refs[mp : mp + dp], refs[mp + dp : mp + 2 * dp]
    z_ref, r_ref, c_ref, q_ref, prev_ref, hs_ref, own_ref, in_own_ref = refs[mp + 2 * dp : mp + 2 * dp + 8]
    x_all, in_all, hid_all, state, low_state, inner, sems = refs[mp + 2 * dp + 8 :]
    t, q = pl.program_id(0), pl.program_id(1)
    slots, width = z_ref.shape[1:]
    full = width * mp
    cols = pl.ds(pl.multiple_of(q * width, width), width)
    x_in = col_copies(x_pieces, where_mp, x_all, sems, 0)
    in_in = row_copies(in_pieces, where_dp, in_all, sems, mp)
    hid_in = row_copies(hid_pieces, where_dp, hid_all, sems, mp + dp)

    @pl.when((t == 0) & (q == 0))
    def _():
        start(x_in)
        start(in_in)
        start(hid_in)
        state[...] = jnp.zeros_like(state)
        finish(x_in)
        finish(in_in)
        for g in range(3):
            rows = pl.ds(pl.multiple_of(g * full + me_ref[0] * width, width), width)
            in_own_ref[g] = in_all[rows, :]

    @pl.when((t == 1) & (q == 0))
    def _():
        finish(hid_in)

    @pl.when(q == 0)
    def _():
        low_state[...] = (state[...] * keep_ref[0]).astype(BF)

    x = x_all[pl.ds(pl.multiple_of(t * slots, slots), slots), :]
    gi = [
        jnp.dot(x, in_all[g * full : (g + 1) * full, cols], preferred_element_type=F32)
        + bias_ref[g : g + 1, :]
        for g in range(3)
    ]
    z_ref[0] = gi[0]
    r_ref[0] = gi[1]
    inner[...] = jnp.broadcast_to(bias_ref[3:4, :], inner.shape)

    @pl.when(t > 0)
    def _():
        low_prev = low_state[...]
        for g, ref in ((0, z_ref.at[0]), (1, r_ref.at[0]), (2, inner)):
            ref[...] += jnp.dot(
                low_prev, hid_all[g * full : (g + 1) * full, cols], preferred_element_type=F32
            )

    prev = state[:, cols] * keep_ref[0]
    z = 1.0 / (1.0 + jnp.exp(-z_ref[0]))
    r = 1.0 / (1.0 + jnp.exp(-r_ref[0]))
    c = jnp.tanh(gi[2] + r * inner[...])
    h = (1.0 - z) * prev + z * c
    z_ref[0] = z
    r_ref[0] = r
    c_ref[0] = c
    q_ref[0] = inner[...]
    prev_ref[0] = prev
    shown = h.astype(BF)
    hs_ref[0] = shown
    state[:, cols] = h

    @pl.when(q == me_ref[0])
    def _():
        own_ref[0] = shown


def forward(steps, slots, width, me, where_mp, where_dp, keep, bias_all, x_pieces, in_pieces, hid_pieces):
    mp, dp = len(x_pieces), len(in_pieces)
    full = mp * width
    tile = pl.BlockSpec((1, slots, width), lambda t, q: (t, 0, q))
    later = pl.BlockSpec(
        (1, slots, width), lambda t, q: (jnp.maximum(t - 1, 0), 0, jnp.where(t == 0, 0, q))
    )
    shape = lambda count, dtype: jax.ShapeDtypeStruct((count, slots, full), dtype)
    return pl.pallas_call(
        functools.partial(forward_kernel, mp, dp),
        grid=(steps, mp),
        in_specs=[IN_SMEM] * 3
        + [
            pl.BlockSpec((1, slots, 1), lambda t, q: (t, 0, 0)),
            pl.BlockSpec((8, width), lambda t, q: (0, q)),
        ]
        + [ANYWHERE] * (mp + 2 * dp),
        out_specs=[
            tile,
            tile,
            tile,
            later,
            later,
            tile,
            pl.BlockSpec((1, slots, width), lambda t, q: (t, 0, 0)),
            pl.BlockSpec((3, width, full), lambda t, q: (0, 0, 0)),
        ],
        out_shape=[shape(steps, F32)] * 3
        + [shape(steps - 1, F32)] * 2
        + [
            shape(steps, BF),
            jax.ShapeDtypeStruct((steps, slots, width), BF),
            jax.ShapeDtypeStruct((3, width, full), BF),
        ],
        scratch_shapes=[
            pltpu.VMEM((steps * slots, full), BF),
            pltpu.VMEM((3 * full, full), BF),
            pltpu.VMEM((3 * full, full), BF),
            pltpu.VMEM((slots, full), F32),
            pltpu.VMEM((slots, full), BF),
            pltpu.VMEM((slots, width), F32),
            pltpu.SemaphoreType.DMA((mp + 2 * dp,)),
        ],
        compiler_params=pltpu.CompilerParams(vmem_limit_bytes=48 * MIB),
        cost_estimate=pl.CostEstimate(
            flops=2 * 6 * steps * slots * full * full,
            bytes_accessed=steps * full * (slots * 24 + full * 12),
            transcendentals=3 * steps * slots * full,
        ),
    )(me, where_mp, where_dp, keep, bias_all, *x_pieces, *in_pieces, *hid_pieces)


def score_kernel(rows, mp, dp, where_mp, hs_ref, one_ref, weight_ref, *refs):
    tgt_pieces, neg_pieces = refs[:mp], refs[mp : mp + dp]
    ds_ref, dhs_ref, du_ref, loss_ref, s_ref, tgt_all, neg_all, sems = refs[mp + dp :]
    i = pl.program_id(0)
    tile = hs_ref.shape[0]
    tgt_in = col_copies(tgt_pieces, where_mp, tgt_all, sems, 0)
    neg_in = row_copies(neg_pieces, None, neg_all, sems, mp)

    @pl.when(i == 0)
    def _():
        start(neg_in)
        start(tgt_in)
        loss_ref[...] = jnp.zeros_like(loss_ref)
        finish(neg_in)

    s_ref[...] = lax.dot_general(
        hs_ref[...] + one_ref[...], neg_all[...], (((1,), (1,)), ((), ())), preferred_element_type=F32
    )

    @pl.when(i == 0)
    def _():
        finish(tgt_in)

    def chunk(j, _):
        at = pl.ds(pl.multiple_of(j * rows, rows), rows)
        s = s_ref[at, :]
        w = weight_ref[at, :]
        tgt = tgt_all[pl.ds(pl.multiple_of(i * tile + j * rows, rows), rows), :].astype(F32)
        u = jnp.sum((hs_ref[at, :] + one_ref[...]).astype(F32) * tgt, axis=1, keepdims=True)
        top = jnp.max(s, axis=1, keepdims=True)
        e = jnp.exp(s - top)
        above = 1.0 / (1.0 + jnp.exp(s - u))
        ea = e * above
        inv = 1.0 / jnp.sum(e, axis=1, keepdims=True)
        mixture = jnp.sum(ea, axis=1, keepdims=True) * inv
        spread = jnp.sum(e * s * s, axis=1, keepdims=True) * inv
        slope = jnp.sum(ea * (1.0 - above), axis=1, keepdims=True) * inv
        shift = s + 1.0
        ds = (w * inv * e) * (bpr_weight * (shift * shift - spread) - above * above * (1.0 / mixture))
        ds_ref[at, :] = ds.astype(BF)
        du_ref[at, :] = (-w * slope / mixture).astype(BF).astype(F32)
        loss_ref[...] += jnp.broadcast_to(
            jnp.sum(w * (-jnp.log(mixture) + bpr_weight * spread), keepdims=True), loss_ref.shape
        )
        return 0

    lax.fori_loop(0, tile // rows, chunk, 0)
    own = pl.ds(pl.multiple_of(i * tile, tile), tile)
    dhs_ref[...] = jnp.dot(ds_ref[...], neg_all[...], preferred_element_type=F32) + du_ref[
        ...
    ] * tgt_all[own, :].astype(F32)


def scores(tile, where_mp, shown, one_row, weight, tgt_pieces, neg_pieces):
    events, full = shown.shape
    mp, dp = len(tgt_pieces), len(neg_pieces)
    count = dp * neg_pieces[0].shape[0]
    row_tile = lambda w: pl.BlockSpec((tile, w), lambda i: (i, 0))
    return pl.pallas_call(
        functools.partial(score_kernel, 32, mp, dp),
        grid=(events // tile,),
        in_specs=[IN_SMEM, row_tile(full), pl.BlockSpec((1, full), lambda i: (0, 0)), row_tile(1)]
        + [ANYWHERE] * (mp + dp),
        out_specs=[row_tile(count), row_tile(full), row_tile(1), pl.BlockSpec((8, 128), lambda i: (0, 0))],
        out_shape=[
            jax.ShapeDtypeStruct((events, count), BF),
            jax.ShapeDtypeStruct((events, full), F32),
            jax.ShapeDtypeStruct((events, 1), F32),
            jax.ShapeDtypeStruct((8, 128), F32),
        ],
        scratch_shapes=[
            pltpu.VMEM((tile, count), F32),
            pltpu.VMEM((events, full), BF),
            pltpu.VMEM((count, full), BF),
            pltpu.SemaphoreType.DMA((mp + dp,)),
        ],
        compiler_params=pltpu.CompilerParams(vmem_limit_bytes=48 * MIB),
        cost_estimate=pl.CostEstimate(
            flops=4 * events * full * count,
            bytes_accessed=events * (full * 8 + count * 2) + count * full * 2,
            transcendentals=3 * events * count,
        ),
    )(where_mp, shown, one_row, weight, *tgt_pieces, *neg_pieces)


def backward_kernel(
    dp, me_ref, where_dp, z_ref, r_ref, c_ref, q_ref, prev_ref, keep_ref, dhs_ref, bias_ref, in_ref, *refs
):
    hid_pieces = refs[:dp]
    dx_ref, own_ref, sum_ref, later, back, hid_all, sems = refs[dp:]
    i, q = pl.program_id(0), pl.program_id(1)
    last_step, last_part = pl.num_programs(0) - 1, pl.num_programs(1) - 1
    width = z_ref.shape[2]
    full = hid_all.shape[1]
    cols = pl.ds(pl.multiple_of(q * width, width), width)
    hid_in = row_copies(hid_pieces, where_dp, hid_all, sems, 0)

    @pl.when((i == 0) & (q == 0))
    def _():
        start(hid_in)
        later[...] = jnp.zeros_like(later)
        sum_ref[...] = jnp.zeros_like(sum_ref)
        finish(hid_in)

    @pl.when(q == 0)
    def _():
        dx_ref[...] = jnp.zeros_like(dx_ref)
        back[...] = jnp.zeros_like(back)

    z, r, c = z_ref[0], r_ref[0], c_ref[0]
    begun = i < last_step
    inner = jnp.where(begun, q_ref[0], jnp.broadcast_to(bias_ref[3:4, :], z.shape))
    prev = jnp.where(begun, prev_ref[0], 0.0)
    dh = later[:, cols] + dhs_ref[...]
    rest = 1.0 - z
    dz = dh * (c - prev) * z * rest
    da = dh * z * (1.0 - c * c)
    dr = da * inner * r * (1.0 - r)
    dq = da * r
    grads = (dz, dr, da, dq)
    zl, rl, al, ql = [v.astype(BF) for v in grads]
    over = (((1,), (1,)), ((), ()))
    dx = lax.dot_general(zl, in_ref[0], over, preferred_element_type=F32)
    dx += lax.dot_general(rl, in_ref[1], over, preferred_element_type=F32)
    dx += lax.dot_general(al, in_ref[2], over, preferred_element_type=F32)
    dx_ref[...] += dx

    @pl.when(begun)
    def _():
        hid = lambda g: hid_all[g * full : (g + 1) * full, cols]
        total = lax.dot_general(zl, hid(0), over, preferred_element_type=F32)
        total += lax.dot_general(rl, hid(1), over, preferred_element_type=F32)
        total += lax.dot_general(ql, hid(2), over, preferred_element_type=F32)
        back[...] += total
        back[:, cols] += dh * rest

    @pl.when(q == me_ref[0])
    def _():
        for k, value in enumerate((zl, rl, al, ql)):
            own_ref[:, k * width : (k + 1) * width] = value
            sum_ref[k : k + 1, :] += jnp.sum(grads[k], axis=0, keepdims=True)

    @pl.when(q == last_part)
    def _():
        later[...] = back[...] * keep_ref[0]


def backward(width, me, where_dp, z, r, c, inner, prev, keep, dhs, bias_all, in_own, hid_pieces):
    steps, slots, full = z.shape
    dp = len(hid_pieces)
    parts = full // width
    tile = pl.BlockSpec((1, slots, width), lambda i, q: (steps - 1 - i, 0, q))
    later = pl.BlockSpec(
        (1, slots, width),
        lambda i, q: (jnp.maximum(steps - 2 - i, 0), 0, jnp.where(i == steps - 1, parts - 1, q)),
    )
    row = lambda w: pl.BlockSpec((slots, w), lambda i, q: (steps - 1 - i, 0))
    return pl.pallas_call(
        functools.partial(backward_kernel, dp),
        grid=(steps, parts),
        in_specs=[IN_SMEM] * 2
        + [tile] * 3
        + [later] * 2
        + [
            pl.BlockSpec((1, slots, 1), lambda i, q: (steps - 1 - i, 0, 0)),
            pl.BlockSpec((slots, width), lambda i, q: (steps - 1 - i, q)),
            pl.BlockSpec((8, width), lambda i, q: (0, q)),
            pl.BlockSpec((3, width, width), lambda i, q: (0, 0, q)),
        ]
        + [ANYWHERE] * dp,
        out_specs=[row(width), row(4 * width), pl.BlockSpec((8, width), lambda i, q: (0, 0))],
        out_shape=[
            jax.ShapeDtypeStruct((steps * slots, width), F32),
            jax.ShapeDtypeStruct((steps * slots, 4 * width), BF),
            jax.ShapeDtypeStruct((8, width), F32),
        ],
        scratch_shapes=[
            pltpu.VMEM((slots, full), F32),
            pltpu.VMEM((slots, full), F32),
            pltpu.VMEM((3 * full, full), BF),
            pltpu.SemaphoreType.DMA((dp,)),
        ],
        compiler_params=pltpu.CompilerParams(vmem_limit_bytes=48 * MIB),
        cost_estimate=pl.CostEstimate(
            flops=2 * steps * slots * full * (3 * full + 3 * width),
            bytes_accessed=steps * full * (slots * 24 + full * 6),
            transcendentals=0,
        ),
    )(me, where_dp, z, r, c, inner, prev, keep, dhs, bias_all, in_own, *hid_pieces)


def weights_kernel(units, mp, order_ref, where_mp, hs_ref, keep_ref, own_ref, sum_ref, loss_ref, *refs):
    x_pieces = refs[:mp]
    kept_ref, sent_ref, total, x_all, sems = refs[mp:]
    x_in = col_copies(x_pieces, where_mp, x_all, sems, 0)
    start(x_in)
    width = sum_ref.shape[1]
    events = x_all.shape[0]
    slots = hs_ref.shape[1]
    over = (((0,), (0,)), ((), ()))
    three = 3 * width
    part = jnp.zeros((total.shape[0], three), F32)
    for t in range(events // slots - 1):
        hb = (hs_ref[t].astype(F32) * keep_ref[t + 1]).astype(BF)
        rows = slice((t + 1) * slots, (t + 2) * slots)
        state = jnp.concatenate([own_ref[rows, : 2 * width], own_ref[rows, three:]], axis=1)
        part += lax.dot_general(hb, state, over, preferred_element_type=F32)
    total[:, three:] = part
    finish(x_in)
    total[:, :three] = lax.dot_general(x_all[...], own_ref[:, :three], over, preferred_element_type=F32)
    for k in range(3):
        total[units : units + 1, k * width : (k + 1) * width] = sum_ref[k : k + 1, :]
    total[units + 1 : units + 2, :width] = sum_ref[3:4, :]
    total[units + 1 : units + 2, width : width + 128] = loss_ref[0:1, :]
    rows = kept_ref.shape[1]
    for k in range(kept_ref.shape[0]):
        for ref, at in ((kept_ref, 2 * k), (sent_ref, 2 * k + 1)):
            ref[k] = total[pl.ds(pl.multiple_of(order_ref[at] * rows, rows), rows), :]


def weight_grads(units, order, where_mp, hs, keep, own, sums, loss, x_pieces):
    mp = len(x_pieces)
    events, width = own.shape[0], sums.shape[1]
    full = hs.shape[2]
    count = order.shape[0]
    half = jax.ShapeDtypeStruct((count // 2, full // count, 6 * width), F32)
    return pl.pallas_call(
        functools.partial(weights_kernel, units, mp),
        in_specs=[IN_SMEM] * 2 + [IN_VMEM] * 5 + [ANYWHERE] * mp,
        out_specs=[IN_VMEM, IN_VMEM],
        out_shape=[half, half],
        scratch_shapes=[
            pltpu.VMEM((full, 6 * width), F32),
            pltpu.VMEM((events, full), BF),
            pltpu.SemaphoreType.DMA((mp,)),
        ],
        compiler_params=pltpu.CompilerParams(vmem_limit_bytes=56 * MIB),
        cost_estimate=pl.CostEstimate(
            flops=2 * events * full * 6 * width,
            bytes_accessed=events * full * 4 + full * 24 * width,
            transcendentals=0,
        ),
    )(order, where_mp, hs, keep, own, sums, loss, *x_pieces)


def output_kernel(units, where_dp, *refs):
    dp = len(refs) - 7
    pieces = refs[:dp]
    in_ref, hid_ref, gate_ref, cand_ref, loss_ref, total, sems = refs[dp:]
    copies = row_copies(pieces, where_dp, total, sems, 0)
    start(copies)
    finish(copies)
    width = total.shape[1] // 6
    for k, ref in enumerate((in_ref, hid_ref)):
        for g in range(3):
            at = (3 * k + g) * width
            for q in range(total.shape[0] // width):
                ref[g, q * units : (q + 1) * units, :] = total[q * width : q * width + units, at : at + units]
    for g in range(3):
        gate_ref[g : g + 1, :] = total[units : units + 1, g * width : g * width + units]
    cand_ref[...] = total[units + 1 : units + 2, :units]
    loss_ref[...] = total[units + 1 : units + 2, width : width + 128]


def outputs(units, mp, where_dp, pieces):
    rows, cols = pieces[0].shape
    dp = len(pieces)
    grad = jax.ShapeDtypeStruct((3, mp * units, units), F32)
    return pl.pallas_call(
        functools.partial(output_kernel, units),
        in_specs=[IN_SMEM] + [ANYWHERE] * dp,
        out_specs=[IN_VMEM] * 5,
        out_shape=[
            grad,
            grad,
            jax.ShapeDtypeStruct((3, units), F32),
            jax.ShapeDtypeStruct((1, units), F32),
            jax.ShapeDtypeStruct((1, 128), F32),
        ],
        scratch_shapes=[pltpu.VMEM((rows * dp, cols), F32), pltpu.SemaphoreType.DMA((dp,))],
        compiler_params=pltpu.CompilerParams(vmem_limit_bytes=48 * MIB),
        cost_estimate=pl.CostEstimate(
            flops=0, bytes_accessed=8 * rows * dp * cols, transcendentals=0
        ),
    )(where_dp, *pieces)


def swap(value, k, axis):
    count = lax.axis_size(axis)
    return lax.ppermute(value, axis, [(i, i ^ k) for i in range(count)])


def gather_mp(value):
    count = lax.axis_size("mp")
    if count != 4:
        return [value] + [swap(value, k, "mp") for k in range(1, count)]
    near = swap(value, 1, "mp")
    middle = lax.ppermute(value, "mp", [(1, 2), (2, 1)])
    over = swap(value, 2, "mp")
    far = lax.ppermute(over, "mp", [(1, 0), (2, 3)])
    place_now = lax.axis_index("mp")
    inside = (place_now == 1) | (place_now == 2)
    return [value, near, over, jnp.where(inside, middle, far)]


def gather_dp(value):
    count = lax.axis_size("dp")
    chips = [value] + [swap(value, k, "dp") for k in range(2, count, 2)]
    other = [swap(piece, 1, "dp") for piece in chips]
    return [piece for pair in zip(chips, other) for piece in pair]


def reduce_dp(kept, sent):
    mine = kept + swap(sent, 1, "dp")
    total = mine[0]
    for k in range(1, mine.shape[0]):
        total = total + swap(mine[k], 2 * k, "dp")
    return total


def low(value):
    return lax.reduce_precision(value, 8, 7).astype(BF)


def on_device(
    item_ids,
    session_ends,
    negatives,
    embedding,
    in_weight,
    hid_weight,
    gate_bias,
    cand_bias,
    out_table,
    out_bias,
):
    dp, mp = lax.axis_size("dp"), lax.axis_size("mp")
    me_dp, me_mp = lax.axis_index("dp"), lax.axis_index("mp")
    order_dp = me_dp ^ jnp.arange(dp, dtype=jnp.int32)
    order_mp = me_mp ^ jnp.arange(mp, dtype=jnp.int32)
    me = me_mp.astype(jnp.int32).reshape(1)
    steps, slots = session_ends.shape
    events = steps * slots
    feats, vocab = embedding.shape
    units = hid_weight.shape[2]
    width = up(units, 128)
    full = mp * width
    neg_count = negatives.shape[0]
    neg_share = neg_count // dp

    end_float = session_ends.astype(F32)
    keep = jnp.concatenate([jnp.zeros((1, slots), F32), 1.0 - end_float[:-1]], axis=0)
    weight = ((1.0 - end_float) / (steps * slots * dp)).reshape(events, 1)
    sources = item_ids[:-1].reshape(events)
    targets = item_ids[1:].reshape(events)
    own_negs = lax.dynamic_slice_in_dim(negatives, me_dp * neg_share, neg_share)

    def padded_rows(value):
        value = value.reshape(3, mp, units, units)
        value = jnp.pad(value, ((0, 0), (0, 0), (0, width - units), (0, width - units)))
        return value.reshape(3 * full, width)

    share = 3 * full // dp
    in_share = lax.dynamic_slice_in_dim(padded_rows(in_weight), me_dp * share, share)
    hid_share = lax.dynamic_slice_in_dim(padded_rows(hid_weight), me_dp * share, share)
    biases = jnp.pad(
        jnp.concatenate([gate_bias, cand_bias[None]]), ((0, 0), (0, width - units))
    )
    first = low(biases)
    second = low(biases - first.astype(F32))
    third = low(biases - first.astype(F32) - second.astype(F32))
    bias_rows = jnp.concatenate([first, second, third, jnp.zeros((4, width), BF)])
    cols = gather_mp(jnp.concatenate([in_share, hid_share, bias_rows]))
    bias_all = place(cols, order_mp, 1, 2 * share, 16)[:12].astype(F32)
    bias_all = jnp.pad(bias_all[0:4] + bias_all[4:8] + bias_all[8:12], ((0, 4), (0, 0)))
    in_pieces = gather_dp(place(cols, order_mp, 1, 0, share))
    hid_pieces = gather_dp(place(cols, order_mp, 1, share, share))

    x_rows, x_sid, x_order = lookup(sources, embedding)
    x_pieces = gather_mp(x_rows[:events])
    t_rows, t_sid, t_order = lookup(jnp.concatenate([targets, own_negs]), out_table, out_bias)
    t_pieces = gather_mp(t_rows[: events + neg_share])
    neg_pieces = gather_dp(place(t_pieces, order_mp, 1, events, neg_share))
    gap = ((0, 0), (0, t_sid.shape[1] - x_sid.shape[1]))
    lists = jnp.concatenate([jnp.pad(x_sid, gap), jnp.pad(x_order, gap), t_sid, t_order])
    lists = jnp.stack(gather_dp(lists.astype(jnp.int32)))
    x_lists = lists[:, 0:2, : x_sid.shape[1]]
    t_lists = lists[:, 2:4]

    keep = keep[:, :, None]
    z, r, c, inner, prev, hs, own_shown, in_own = forward(
        steps, slots, width, me, order_mp, order_dp, keep, bias_all, x_pieces, in_pieces, hid_pieces
    )
    shown = hs.reshape(events, full)
    own_shown = own_shown.reshape(events, width)
    rows_all = gather_dp(own_shown)
    col = jnp.arange(full)[None, :]
    one_row = ((col >= units) & (col < units + 3)).astype(BF)
    neg_low, dhs, tgt_low, loss = scores(slots, order_mp, shown, one_row, weight, t_pieces, neg_pieces)

    counted = jnp.where(jnp.arange(width)[None, :] == units, BF(1.0), own_shown)
    neg_table = jnp.einsum("nj,nh->jh", neg_low, counted, preferred_element_type=F32)
    neg_table = neg_table.reshape(dp // 2, 2, neg_share, width)
    neg_sum = reduce_dp(neg_table[:, 0], neg_table[:, 1])
    scale_rows = up(-(-events // width), 8)
    scale = jnp.pad(tgt_low.reshape(events), (0, scale_rows * width - events))
    neg_all = gather_dp(jnp.concatenate([neg_sum, scale.reshape(scale_rows, width)]))
    scale_all = jnp.stack([v[neg_share:].reshape(-1)[:events] for v in neg_all])
    scale_all = jnp.concatenate([scale_all, jnp.ones((dp, neg_share), F32)], axis=1)

    dx, own, sums = backward(
        width, me, order_dp, z, r, c, inner, prev, keep, dhs, bias_all, in_own, hid_pieces
    )
    dx_all = gather_dp(dx)
    kept, sent = weight_grads(units, order_dp, order_mp, hs, keep, own, sums, loss, x_pieces)
    in_sum, hid_sum, gate_sum, cand_sum, loss_sum = outputs(
        units, mp, order_dp, gather_dp(reduce_dp(kept, sent))
    )

    items = vocab // dp
    base = (me_dp * items).astype(jnp.int32)
    table_sum, bias_sum = scatter(
        base, units, items, t_lists, rows_all, scale_all, [v[:neg_share] for v in neg_all]
    )
    (embed_sum,) = scatter(base, units, items, x_lists, dx_all)
    return (
        loss_sum[0, 0],
        in_sum,
        hid_sum,
        gate_sum,
        cand_sum.reshape(units),
        embed_sum,
        table_sum,
        bias_sum.reshape(items),
    )


def solution(mesh):
    return jax.shard_map(
        on_device,
        mesh=mesh,
        in_specs=(
            P(None, "dp"),
            P(None, "dp"),
            P(),
            P("mp", None),
            P(None, None, "mp"),
            P(None, None, "mp"),
            P(None, "mp"),
            P("mp"),
            P("mp", None),
            P(),
        ),
        out_specs=(
            P(),
            P(None, None, "mp"),
            P(None, None, "mp"),
            P(None, "mp"),
            P("mp"),
            P("mp", "dp"),
            P("mp", "dp"),
            P("dp"),
        ),
        check_vma=False,
    )
```

```python
import functools
import math

import jax
import jax.numpy as jnp
from jax import lax
from jax.experimental import pallas as pl
from jax.experimental.pallas import tpu as pltpu
from jax.sharding import PartitionSpec as P

bpr_weight = 1.0
BF = jnp.bfloat16
F32 = jnp.float32
ITEM_BLOCK = 4096
CHUNK = 256
MIB = 1024 * 1024
ANYWHERE = pl.BlockSpec(memory_space=pl.ANY)
IN_SMEM = pl.BlockSpec(memory_space=pltpu.SMEM)
IN_VMEM = pl.BlockSpec(memory_space=pltpu.VMEM)


def up(count, unit):
    return -(-count // unit) * unit


def lookup_kernel(has_bias, feats, cnt_ref, idr_ref, idc_ref, tab_ref, *rest):
    rest = list(rest)
    bias_ref = rest.pop(0) if has_bias else None
    sid, order, perm, xs, held, sems = rest[-6:]
    outs = rest[:-6]
    count = idr_ref.shape[1]
    blocks, _, width = held.shape

    def fetch(b):
        return pltpu.make_async_copy(
            tab_ref.at[:, pl.ds(b * width, width)], held.at[b], sems.at[b]
        )

    for b in range(blocks):
        fetch(b).start()
    lane = lax.broadcasted_iota(jnp.int32, (CHUNK, count), 1)
    keyr = idr_ref[...] * 4096 + lax.broadcasted_iota(jnp.int32, (1, count), 1)
    sid[...] = jnp.zeros_like(sid)
    order[...] = jnp.zeros_like(order)

    def sort_rows(i, _):
        rows = pl.ds(pl.multiple_of(i * CHUNK, CHUNK), CHUNK)
        idc = idc_ref[rows, :]
        at = i * CHUNK + lax.broadcasted_iota(jnp.int32, (CHUNK, 1), 0)
        keyc = idc * 4096 + at
        rank = jnp.sum((keyr < keyc).astype(F32), axis=1, keepdims=True).astype(jnp.int32)
        hit = rank == lane
        perm[rows, :] = hit.astype(F32).astype(BF)
        sid[...] += jnp.sum(jnp.where(hit, idc, 0).astype(F32), axis=0, keepdims=True)
        order[...] += jnp.sum(jnp.where(hit, at, 0).astype(F32), axis=0, keepdims=True)
        return 0

    lax.fori_loop(0, count // CHUNK, sort_rows, 0)
    xs[...] = jnp.zeros_like(xs)
    for b in range(blocks):
        fetch(b).wait()
        base = b * width

        def pick_chunk(c, _, b=b, base=base):
            cols = pl.ds(pl.multiple_of(c * CHUNK, CHUNK), CHUNK)
            ids = sid[:, cols].astype(jnp.int32) - base
            pick = (lax.broadcasted_iota(jnp.int32, (width, CHUNK), 0) == ids).astype(F32).astype(BF)
            xs[0:feats, cols] += jnp.dot(held[b], pick, preferred_element_type=F32)
            return 0

        lax.fori_loop(
            cnt_ref[b] // CHUNK, (cnt_ref[b + 1] + CHUNK - 1) // CHUNK, pick_chunk, 0
        )
    out = lax.dot_general(
        perm[...], xs[...].astype(BF), (((1,), (1,)), ((), ())), preferred_element_type=F32
    )
    if has_bias:
        value = bias_ref[...]
        first = value.astype(BF).astype(F32)
        second = (value - first).astype(BF).astype(F32)
        parts = (first, second, value - first - second)
        groups = value.shape[0]
        idc = idc_ref[...]
        group = (idc // 128 == lax.broadcasted_iota(jnp.int32, (count, groups), 1)).astype(F32).astype(BF)
        member = lax.broadcasted_iota(jnp.int32, (count, 128), 1) == idc % 128
        col = lax.broadcasted_iota(jnp.int32, out.shape, 1)
        for k, part in enumerate(parts):
            near = jnp.dot(group, part.astype(BF), preferred_element_type=F32)
            own = jnp.sum(jnp.where(member, near, 0.0), axis=1, keepdims=True)
            out = jnp.where(col == feats + k, own, out)
    at = 0
    for ref in outs:
        ref[...] = out[at : at + ref.shape[0]].astype(BF)
        at += ref.shape[0]


def lookup(parts, table, bias=None):
    ids = jnp.concatenate(parts)
    feats, vocab = table.shape
    width = up(feats, 128)
    count = ids.shape[0]
    padded = up(count, CHUNK)
    ids = jnp.concatenate([ids, jnp.full((padded - count,), vocab, jnp.int32)])
    blocks = vocab // ITEM_BLOCK
    edges = jnp.arange(blocks + 1, dtype=jnp.int32) * ITEM_BLOCK
    cnt = jnp.sum((ids[None, :] < edges[:, None]).astype(jnp.int32), axis=1)
    vmem = pl.BlockSpec(memory_space=pltpu.VMEM)
    in_specs = [pl.BlockSpec(memory_space=pltpu.SMEM), vmem, vmem, pl.BlockSpec(memory_space=pl.ANY)]
    args = [cnt, ids.reshape(1, padded), ids.reshape(padded, 1), table]
    if bias is not None:
        in_specs.append(vmem)
        args.append(bias.reshape(vocab // 128, 128))
    return pl.pallas_call(
        functools.partial(lookup_kernel, bias is not None, feats),
        in_specs=in_specs,
        out_specs=[vmem] * (len(parts) + 2),
        scratch_shapes=[
            pltpu.VMEM((padded, padded), BF),
            pltpu.VMEM((width, padded), F32),
            pltpu.VMEM((blocks, feats, ITEM_BLOCK), BF),
            pltpu.SemaphoreType.DMA((blocks,)),
        ],
        out_shape=[
            *[jax.ShapeDtypeStruct((part.shape[0], width), BF) for part in parts],
            jax.ShapeDtypeStruct((1, padded), F32),
            jax.ShapeDtypeStruct((1, padded), F32),
        ],
        compiler_params=pltpu.CompilerParams(vmem_limit_bytes=56 * MIB),
        cost_estimate=pl.CostEstimate(
            flops=2 * vocab * feats * 512, bytes_accessed=vocab * feats * 2, transcendentals=0
        ),
    )(*args)


def scatter_kernel(feats, sources, plan, neg_plan, base_ref, edge_ref, list_ref, *refs):
    refs = list(refs)
    scaled = neg_plan is not None
    scale_ref = refs.pop(0) if scaled else None
    blocks = [refs.pop(0) for _ in plan]
    negs = [refs.pop(0) for _ in neg_plan or ()]
    out_ref = refs.pop(0)
    bias_ref = refs.pop(0) if scaled else None
    total, held, sems = refs[:3]
    base = base_ref[0]
    items, width = total.shape
    each = held.shape[0] // sources
    if scaled:
        low_rows = refs[3]
        depth = low_rows.shape[0] // sources
        copies = block_copies(plan, depth, blocks, None, low_rows, sems, 0)
        neg_rows = [(k, depth + row) for k, row in neg_plan]
        copies += block_copies(neg_rows, each, negs, None, held, sems, len(plan), (0, each - depth))
    else:
        copies = block_copies(plan, each, blocks, None, held, sems, 0)
    start(copies)
    total[...] = jnp.zeros_like(total)
    finish(copies)
    if scaled:

        def widen(s, _):
            for at in range(0, depth, 128):
                rows = min(128, depth - at)
                wide = low_rows[pl.ds(pl.multiple_of(s * depth + at, 128), rows), :].astype(F32)
                col = lax.broadcasted_iota(jnp.int32, wide.shape, 1)
                held[pl.ds(pl.multiple_of(s * each + at, 64), rows), :] = jnp.where(col == feats, 1.0, wide)
            return 0

        lax.fori_loop(0, sources, widen, 0)

    def term(s, r):
        row = list_ref[s, 1, r]
        value = held[pl.ds(s * each + row, 1), :]
        return value * scale_ref[s, row] if scaled else value

    for s in range(sources):
        first, last = edge_ref[s, 0], edge_ref[s, 1]

        @pl.when(last > first)
        def _(s=s, first=first, last=last):
            item = list_ref[s, 0, first] - base
            value = total[pl.ds(item, 1), :] + term(s, first)

            def add(r, carry):
                item, value = carry
                new = list_ref[s, 0, r] - base
                ahead = total[pl.ds(new, 1), :]
                total[pl.ds(item, 1), :] = value
                return new, jnp.where(new == item, value, ahead) + term(s, r)

            item, value = lax.fori_loop(first + 1, last, add, (item, value))
            total[pl.ds(item, 1), :] = value

    tile = 512 if items % 512 == 0 else 128
    for at in range(0, items, tile):
        turned = total[at : at + tile, :].T
        out_ref[:, at : at + tile] = turned[:feats]
        if scaled:
            bias_ref[:, at : at + tile] = turned[feats : feats + 1]


def scatter(base, feats, items, lists, depth, plan, blocks, scale=None, neg_share=0, neg_plan=None, negs=()):
    width = blocks[0].shape[-1]
    sources = lists.shape[0]
    each = depth + neg_share
    below = lambda v: jnp.sum((lists[:, 0] < v).astype(jnp.int32), axis=1)
    edges = jnp.stack([below(base), below(base + items)], axis=1)
    scaled = scale is not None
    out_shape = [jax.ShapeDtypeStruct((feats, items), F32)]
    scratch = [
        pltpu.VMEM((items, width), F32),
        pltpu.VMEM((sources * each, width), F32),
        pltpu.SemaphoreType.DMA((len(blocks) + len(negs),)),
    ]
    if scaled:
        out_shape.append(jax.ShapeDtypeStruct((1, items), F32))
        scratch.append(pltpu.VMEM((sources * depth, width), BF))
    return pl.pallas_call(
        functools.partial(scatter_kernel, feats, sources, plan, neg_plan),
        in_specs=[IN_SMEM] * (4 if scaled else 3) + [ANYWHERE] * (len(blocks) + len(negs)),
        out_specs=[IN_VMEM] * len(out_shape),
        out_shape=out_shape,
        scratch_shapes=scratch,
        compiler_params=pltpu.CompilerParams(vmem_limit_bytes=56 * MIB),
        cost_estimate=pl.CostEstimate(
            flops=0, bytes_accessed=sources * each * width * 8, transcendentals=0
        ),
    )(base.reshape(1), edges, lists, *([scale] if scaled else []), *blocks, *negs)


def place_kernel(first, axis, where_ref, *refs):
    *pieces, out_ref, sems = refs
    size = out_ref.shape[axis] // len(pieces)
    copies = []
    for k, piece in enumerate(pieces):
        spot = pl.ds(pl.multiple_of(where_ref[k] * size, size), size)
        target = out_ref.at[spot, :] if axis == 0 else out_ref.at[:, spot]
        source = piece.at[pl.ds(first, target.shape[0]), :]
        copies.append(pltpu.make_async_copy(source, target, sems.at[k]))
    for copy in copies:
        copy.start()
    for copy in copies:
        copy.wait()


def place(pieces, where, axis, first=0, rows=None):
    shape = [rows or pieces[0].shape[0], pieces[0].shape[1]]
    shape[axis] *= len(pieces)
    anywhere = pl.BlockSpec(memory_space=pl.ANY)
    return pl.pallas_call(
        functools.partial(place_kernel, first, axis),
        in_specs=[pl.BlockSpec(memory_space=pltpu.SMEM)] + [anywhere] * len(pieces),
        out_specs=pl.BlockSpec(memory_space=pltpu.VMEM),
        scratch_shapes=[pltpu.SemaphoreType.DMA((len(pieces),))],
        out_shape=jax.ShapeDtypeStruct(tuple(shape), pieces[0].dtype),
        compiler_params=pltpu.CompilerParams(vmem_limit_bytes=16 * MIB),
        cost_estimate=pl.CostEstimate(
            flops=0, bytes_accessed=4 * shape[0] * shape[1], transcendentals=0
        ),
    )(where, *pieces)


def block_copies(plan, depth, blocks, where_ref, target, sems, first_sem, window=None):
    copies = []
    for i, (block, (k, row)) in enumerate(zip(blocks, plan)):
        size = block.shape[0]
        source = block
        if window is not None:
            size = window[1]
            source = block.at[pl.ds(window[0], size), :]
        unit = math.gcd(depth, row) if row else depth
        at = pl.multiple_of(where_ref[k] * depth + row, unit) if where_ref is not None else k * depth + row
        copies.append(
            pltpu.make_async_copy(source, target.at[pl.ds(at, size), :], sems.at[first_sem + i])
        )
    return copies


def col_copies(pieces, where_ref, target, sems, first_sem):
    rows = target.shape[0]
    copies = []
    for k, piece in enumerate(pieces):
        size = piece.shape[1]
        spot = pl.ds(pl.multiple_of(where_ref[k] * size, size), size)
        copies.append(
            pltpu.make_async_copy(piece.at[pl.ds(0, rows), :], target.at[:, spot], sems.at[first_sem + k])
        )
    return copies


def start(copies):
    for copy in copies:
        copy.start()


def finish(copies):
    for copy in copies:
        copy.wait()


def forward_kernel(mp, plan, share, me_ref, where_mp, where_dp, keep_ref, bias_ref, *refs):
    count = len(plan)
    x_pieces, blocks = refs[:mp], refs[mp : mp + count]
    z_ref, r_ref, c_ref, q_ref, prev_ref, hs_ref, own_ref, in_own_ref = refs[mp + count : mp + count + 8]
    x_all, in_all, hid_all, state, low_state, inner, sems = refs[mp + count + 8 :]
    t, q = pl.program_id(0), pl.program_id(1)
    slots, width = z_ref.shape[1:]
    full = width * mp
    cols = pl.ds(pl.multiple_of(q * width, width), width)
    x_in = col_copies(x_pieces, where_mp, x_all, sems, 0)
    in_in, hid_in = weight_copies(plan, share, blocks, where_dp, in_all, hid_all, sems, mp)

    @pl.when((t == 0) & (q == 0))
    def _():
        start(x_in)
        start(in_in)
        start(hid_in)
        state[...] = jnp.zeros_like(state)
        finish(x_in)
        finish(in_in)
        for g in range(3):
            rows = pl.ds(pl.multiple_of(g * full + me_ref[0] * width, width), width)
            in_own_ref[g] = in_all[rows, :]

    @pl.when((t == 1) & (q == 0))
    def _():
        finish(hid_in)

    @pl.when(q == 0)
    def _():
        low_state[...] = (state[...] * keep_ref[0]).astype(BF)

    x = x_all[pl.ds(pl.multiple_of(t * slots, slots), slots), :]
    gi = [
        jnp.dot(x, in_all[g * full : (g + 1) * full, cols], preferred_element_type=F32)
        + bias_ref[g : g + 1, :]
        for g in range(3)
    ]
    z_ref[0] = gi[0]
    r_ref[0] = gi[1]
    inner[...] = jnp.broadcast_to(bias_ref[3:4, :], inner.shape)

    @pl.when(t > 0)
    def _():
        low_prev = low_state[...]
        for g, ref in ((0, z_ref.at[0]), (1, r_ref.at[0]), (2, inner)):
            ref[...] += jnp.dot(
                low_prev, hid_all[g * full : (g + 1) * full, cols], preferred_element_type=F32
            )

    prev = state[:, cols] * keep_ref[0]
    z = 1.0 / (1.0 + jnp.exp(-z_ref[0]))
    r = 1.0 / (1.0 + jnp.exp(-r_ref[0]))
    c = jnp.tanh(gi[2] + r * inner[...])
    h = (1.0 - z) * prev + z * c
    z_ref[0] = z
    r_ref[0] = r
    c_ref[0] = c
    q_ref[0] = inner[...]
    prev_ref[0] = prev
    shown = h.astype(BF)
    hs_ref[0] = shown
    state[:, cols] = h

    @pl.when(q == me_ref[0])
    def _():
        own_ref[0] = shown


def weight_copies(plan, share, blocks, where_dp, in_all, hid_all, sems, first_sem):
    split = [[], []]
    for i, (block, (k, row)) in enumerate(zip(blocks, plan)):
        for part in range(2):
            if row <= part * share < row + block.shape[0]:
                split[part].append((i, block.at[pl.ds(part * share - row, share), :], k))
    made = []
    for part, target in enumerate((in_all, hid_all)):
        made.append([])
        for i, source, k in split[part]:
            if target is None:
                continue
            at = pl.multiple_of(where_dp[k] * share, share)
            sem = sems.at[first_sem + 2 * i + part]
            made[part].append(pltpu.make_async_copy(source, target.at[pl.ds(at, share), :], sem))
    return made


def forward(steps, slots, width, me, where_mp, where_dp, keep, bias_all, x_pieces, plan, share, blocks):
    mp, dp = len(x_pieces), len(blocks)
    full = mp * width
    tile = pl.BlockSpec((1, slots, width), lambda t, q: (t, 0, q))
    later = pl.BlockSpec(
        (1, slots, width), lambda t, q: (jnp.maximum(t - 1, 0), 0, jnp.where(t == 0, 0, q))
    )
    shape = lambda count, dtype: jax.ShapeDtypeStruct((count, slots, full), dtype)
    return pl.pallas_call(
        functools.partial(forward_kernel, mp, plan, share),
        grid=(steps, mp),
        in_specs=[IN_SMEM] * 3
        + [
            pl.BlockSpec((1, slots, 1), lambda t, q: (t, 0, 0)),
            pl.BlockSpec((8, width), lambda t, q: (0, q)),
        ]
        + [ANYWHERE] * (mp + dp),
        out_specs=[
            tile,
            tile,
            tile,
            later,
            later,
            tile,
            pl.BlockSpec((1, slots, width), lambda t, q: (t, 0, 0)),
            pl.BlockSpec((3, width, full), lambda t, q: (0, 0, 0)),
        ],
        out_shape=[shape(steps, F32)] * 3
        + [shape(steps - 1, F32)] * 2
        + [
            shape(steps, BF),
            jax.ShapeDtypeStruct((steps, slots, width), BF),
            jax.ShapeDtypeStruct((3, width, full), BF),
        ],
        scratch_shapes=[
            pltpu.VMEM((steps * slots, full), BF),
            pltpu.VMEM((3 * full, full), BF),
            pltpu.VMEM((3 * full, full), BF),
            pltpu.VMEM((slots, full), F32),
            pltpu.VMEM((slots, full), BF),
            pltpu.VMEM((slots, width), F32),
            pltpu.SemaphoreType.DMA((mp + 2 * dp,)),
        ],
        compiler_params=pltpu.CompilerParams(vmem_limit_bytes=48 * MIB),
        cost_estimate=pl.CostEstimate(
            flops=2 * 6 * steps * slots * full * full,
            bytes_accessed=steps * full * (slots * 24 + full * 12),
            transcendentals=3 * steps * slots * full,
        ),
    )(me, where_mp, where_dp, keep, bias_all, *x_pieces, *blocks)


def score_kernel(rows, mp, plan, dp, where_mp, hs_ref, own_ref, one_ref, weight_ref, *refs):
    count = len(plan)
    tgt_pieces, blocks = refs[:mp], refs[mp : mp + count]
    ds_ref, dhs_ref, du_ref, loss_ref, kept_ref, sent_ref, s_ref, tgt_all, neg_all, table, sems = refs[mp + count :]
    i = pl.program_id(0)
    tile = hs_ref.shape[0]
    width, share = kept_ref.shape[1:]
    tgt_in = col_copies(tgt_pieces, where_mp, tgt_all, sems, 0)
    neg_in = block_copies(plan, share, blocks, None, neg_all, sems, mp)

    @pl.when(i == 0)
    def _():
        start(neg_in)
        start(tgt_in)
        loss_ref[...] = jnp.zeros_like(loss_ref)
        table[...] = jnp.zeros_like(table)
        finish(neg_in)

    s_ref[...] = lax.dot_general(
        hs_ref[...] + one_ref[...], neg_all[...], (((1,), (1,)), ((), ())), preferred_element_type=F32
    )

    @pl.when(i == 0)
    def _():
        finish(tgt_in)

    def chunk(j, _):
        at = pl.ds(pl.multiple_of(j * rows, rows), rows)
        s = s_ref[at, :]
        w = weight_ref[at, :]
        tgt = tgt_all[pl.ds(pl.multiple_of(i * tile + j * rows, rows), rows), :].astype(F32)
        u = jnp.sum((hs_ref[at, :] + one_ref[...]).astype(F32) * tgt, axis=1, keepdims=True)
        top = jnp.max(s, axis=1, keepdims=True)
        e = jnp.exp(s - top)
        above = 1.0 / (1.0 + jnp.exp(s - u))
        ea = e * above
        inv = 1.0 / jnp.sum(e, axis=1, keepdims=True)
        mixture = jnp.sum(ea, axis=1, keepdims=True) * inv
        spread = jnp.sum(e * s * s, axis=1, keepdims=True) * inv
        slope = jnp.sum(ea * (1.0 - above), axis=1, keepdims=True) * inv
        shift = s + 1.0
        ds = (w * inv * e) * (bpr_weight * (shift * shift - spread) - above * above * (1.0 / mixture))
        ds_ref[at, :] = ds.astype(BF)
        du_ref[at, :] = (-w * slope / mixture).astype(BF).astype(F32)
        loss_ref[...] += jnp.broadcast_to(
            jnp.sum(w * (-jnp.log(mixture) + bpr_weight * spread), keepdims=True), loss_ref.shape
        )
        return 0

    lax.fori_loop(0, tile // rows, chunk, 0)
    own = pl.ds(pl.multiple_of(i * tile, tile), tile)
    dhs_ref[...] = jnp.dot(ds_ref[...], neg_all[...], preferred_element_type=F32) + du_ref[
        ...
    ] * tgt_all[own, :].astype(F32)
    counted = own_ref[...] + one_ref[:, :width]
    table[...] += lax.dot_general(counted, ds_ref[...], (((0,), (0,)), ((), ())), preferred_element_type=F32)

    @pl.when(i == pl.num_programs(0) - 1)
    def _():
        for k in range(dp // 2):
            kept_ref[k] = table[:, 2 * k * share : (2 * k + 1) * share]
            sent_ref[k] = table[:, (2 * k + 1) * share : (2 * k + 2) * share]


def scores(tile, dp, where_mp, shown, own_shown, one_row, weight, tgt_pieces, plan, blocks):
    events, full = shown.shape
    width = own_shown.shape[1]
    mp = len(tgt_pieces)
    share = blocks[0].shape[0]
    count = dp * share
    row_tile = lambda w: pl.BlockSpec((tile, w), lambda i: (i, 0))
    half = jax.ShapeDtypeStruct((dp // 2, width, share), F32)
    half_spec = pl.BlockSpec((dp // 2, width, share), lambda i: (0, 0, 0))
    return pl.pallas_call(
        functools.partial(score_kernel, 32, mp, plan, dp),
        grid=(events // tile,),
        in_specs=[
            IN_SMEM,
            row_tile(full),
            row_tile(width),
            pl.BlockSpec((1, full), lambda i: (0, 0)),
            row_tile(1),
        ]
        + [ANYWHERE] * (mp + len(blocks)),
        out_specs=[
            pl.BlockSpec((tile, count), lambda i: (0, 0)),
            row_tile(full),
            row_tile(1),
            pl.BlockSpec((8, 128), lambda i: (0, 0)),
            half_spec,
            half_spec,
        ],
        out_shape=[
            jax.ShapeDtypeStruct((tile, count), BF),
            jax.ShapeDtypeStruct((events, full), F32),
            jax.ShapeDtypeStruct((events, 1), F32),
            jax.ShapeDtypeStruct((8, 128), F32),
            half,
            half,
        ],
        scratch_shapes=[
            pltpu.VMEM((tile, count), F32),
            pltpu.VMEM((events, full), BF),
            pltpu.VMEM((count, full), BF),
            pltpu.VMEM((width, count), F32),
            pltpu.SemaphoreType.DMA((mp + len(blocks),)),
        ],
        compiler_params=pltpu.CompilerParams(vmem_limit_bytes=48 * MIB),
        cost_estimate=pl.CostEstimate(
            flops=4 * events * full * count,
            bytes_accessed=events * (full * 8 + count * 2) + count * full * 2,
            transcendentals=3 * events * count,
        ),
    )(where_mp, shown, own_shown, one_row, weight, *tgt_pieces, *blocks)[1:]


def backward_kernel(
    plan, share, me_ref, where_dp, z_ref, r_ref, c_ref, q_ref, prev_ref, keep_ref, dhs_ref, bias_ref, in_ref, *refs
):
    count = len(plan)
    blocks = refs[:count]
    dx_ref, own_ref, sum_ref, later, back, hid_all, sems = refs[count:]
    i, q = pl.program_id(0), pl.program_id(1)
    last_step, last_part = pl.num_programs(0) - 1, pl.num_programs(1) - 1
    width = z_ref.shape[2]
    full = hid_all.shape[1]
    cols = pl.ds(pl.multiple_of(q * width, width), width)
    _, hid_in = weight_copies(plan, share, blocks, where_dp, None, hid_all, sems, 0)

    @pl.when((i == 0) & (q == 0))
    def _():
        start(hid_in)
        later[...] = jnp.zeros_like(later)
        sum_ref[...] = jnp.zeros_like(sum_ref)
        finish(hid_in)

    @pl.when(q == 0)
    def _():
        dx_ref[...] = jnp.zeros_like(dx_ref)
        back[...] = jnp.zeros_like(back)

    z, r, c = z_ref[0], r_ref[0], c_ref[0]
    begun = i < last_step
    inner = jnp.where(begun, q_ref[0], jnp.broadcast_to(bias_ref[3:4, :], z.shape))
    prev = jnp.where(begun, prev_ref[0], 0.0)
    dh = later[:, cols] + dhs_ref[...]
    rest = 1.0 - z
    dz = dh * (c - prev) * z * rest
    da = dh * z * (1.0 - c * c)
    dr = da * inner * r * (1.0 - r)
    dq = da * r
    grads = (dz, dr, da, dq)
    zl, rl, al, ql = [v.astype(BF) for v in grads]
    over = (((1,), (1,)), ((), ()))
    dx = lax.dot_general(zl, in_ref[0], over, preferred_element_type=F32)
    dx += lax.dot_general(rl, in_ref[1], over, preferred_element_type=F32)
    dx += lax.dot_general(al, in_ref[2], over, preferred_element_type=F32)
    dx_ref[...] += dx

    @pl.when(begun)
    def _():
        hid = lambda g: hid_all[g * full : (g + 1) * full, cols]
        total = lax.dot_general(zl, hid(0), over, preferred_element_type=F32)
        total += lax.dot_general(rl, hid(1), over, preferred_element_type=F32)
        total += lax.dot_general(ql, hid(2), over, preferred_element_type=F32)
        back[...] += total
        back[:, cols] += dh * rest

    @pl.when(q == me_ref[0])
    def _():
        for k, value in enumerate((zl, rl, al, ql)):
            own_ref[:, k * width : (k + 1) * width] = value
            sum_ref[k : k + 1, :] += jnp.sum(grads[k], axis=0, keepdims=True)

    @pl.when(q == last_part)
    def _():
        later[...] = back[...] * keep_ref[0]


def backward(width, me, where_dp, z, r, c, inner, prev, keep, dhs, bias_all, in_own, plan, share, blocks):
    steps, slots, full = z.shape
    parts = full // width
    tile = pl.BlockSpec((1, slots, width), lambda i, q: (steps - 1 - i, 0, q))
    later = pl.BlockSpec(
        (1, slots, width),
        lambda i, q: (jnp.maximum(steps - 2 - i, 0), 0, jnp.where(i == steps - 1, parts - 1, q)),
    )
    row = lambda w: pl.BlockSpec((slots, w), lambda i, q: (steps - 1 - i, 0))
    return pl.pallas_call(
        functools.partial(backward_kernel, plan, share),
        grid=(steps, parts),
        in_specs=[IN_SMEM] * 2
        + [tile] * 3
        + [later] * 2
        + [
            pl.BlockSpec((1, slots, 1), lambda i, q: (steps - 1 - i, 0, 0)),
            pl.BlockSpec((slots, width), lambda i, q: (steps - 1 - i, q)),
            pl.BlockSpec((8, width), lambda i, q: (0, q)),
            pl.BlockSpec((3, width, width), lambda i, q: (0, 0, q)),
        ]
        + [ANYWHERE] * len(blocks),
        out_specs=[row(width), row(4 * width), pl.BlockSpec((8, width), lambda i, q: (0, 0))],
        out_shape=[
            jax.ShapeDtypeStruct((steps * slots, width), F32),
            jax.ShapeDtypeStruct((steps * slots, 4 * width), BF),
            jax.ShapeDtypeStruct((8, width), F32),
        ],
        scratch_shapes=[
            pltpu.VMEM((slots, full), F32),
            pltpu.VMEM((slots, full), F32),
            pltpu.VMEM((3 * full, full), BF),
            pltpu.SemaphoreType.DMA((2 * len(blocks),)),
        ],
        compiler_params=pltpu.CompilerParams(vmem_limit_bytes=48 * MIB),
        cost_estimate=pl.CostEstimate(
            flops=2 * steps * slots * full * (3 * full + 3 * width),
            bytes_accessed=steps * full * (slots * 24 + full * 6),
            transcendentals=0,
        ),
    )(me, where_dp, z, r, c, inner, prev, keep, dhs, bias_all, in_own, *blocks)


def weights_kernel(units, mp, order_ref, where_mp, hs_ref, keep_ref, own_ref, sum_ref, loss_ref, *refs):
    x_pieces = refs[:mp]
    kept_ref, sent_ref, total, x_all, sems = refs[mp:]
    x_in = col_copies(x_pieces, where_mp, x_all, sems, 0)
    start(x_in)
    width = sum_ref.shape[1]
    events = x_all.shape[0]
    slots = hs_ref.shape[1]
    over = (((0,), (0,)), ((), ()))
    three = 3 * width
    part = jnp.zeros((total.shape[0], three), F32)
    for t in range(events // slots - 1):
        hb = (hs_ref[t].astype(F32) * keep_ref[t + 1]).astype(BF)
        rows = slice((t + 1) * slots, (t + 2) * slots)
        state = jnp.concatenate([own_ref[rows, : 2 * width], own_ref[rows, three:]], axis=1)
        part += lax.dot_general(hb, state, over, preferred_element_type=F32)
    total[:, three:] = part
    finish(x_in)
    total[:, :three] = lax.dot_general(x_all[...], own_ref[:, :three], over, preferred_element_type=F32)
    for k in range(3):
        total[units : units + 1, k * width : (k + 1) * width] = sum_ref[k : k + 1, :]
    total[units + 1 : units + 2, :width] = sum_ref[3:4, :]
    total[units + 1 : units + 2, width : width + 128] = loss_ref[0:1, :]
    rows = kept_ref.shape[1]
    for k in range(kept_ref.shape[0]):
        for ref, at in ((kept_ref, 2 * k), (sent_ref, 2 * k + 1)):
            ref[k] = total[pl.ds(pl.multiple_of(order_ref[at] * rows, rows), rows), :]


def weight_grads(units, order, where_mp, hs, keep, own, sums, loss, x_pieces):
    mp = len(x_pieces)
    events, width = own.shape[0], sums.shape[1]
    full = hs.shape[2]
    count = order.shape[0]
    half = jax.ShapeDtypeStruct((count // 2, full // count, 6 * width), F32)
    return pl.pallas_call(
        functools.partial(weights_kernel, units, mp),
        in_specs=[IN_SMEM] * 2 + [IN_VMEM] * 5 + [ANYWHERE] * mp,
        out_specs=[IN_VMEM, IN_VMEM],
        out_shape=[half, half],
        scratch_shapes=[
            pltpu.VMEM((full, 6 * width), F32),
            pltpu.VMEM((events, full), BF),
            pltpu.SemaphoreType.DMA((mp,)),
        ],
        compiler_params=pltpu.CompilerParams(vmem_limit_bytes=56 * MIB),
        cost_estimate=pl.CostEstimate(
            flops=2 * events * full * 6 * width,
            bytes_accessed=events * full * 4 + full * 24 * width,
            transcendentals=0,
        ),
    )(order, where_mp, hs, keep, own, sums, loss, *x_pieces)


def output_kernel(units, plan, depth, where_dp, *refs):
    count = len(plan)
    in_ref, hid_ref, gate_ref, cand_ref, loss_ref, total, sems = refs[count:]
    copies = block_copies(plan, depth, refs[:count], where_dp, total, sems, 0)
    start(copies)
    finish(copies)
    width = total.shape[1] // 6
    for k, ref in enumerate((in_ref, hid_ref)):
        for g in range(3):
            at = (3 * k + g) * width
            for q in range(total.shape[0] // width):
                ref[g, q * units : (q + 1) * units, :] = total[q * width : q * width + units, at : at + units]
    for g in range(3):
        gate_ref[g : g + 1, :] = total[units : units + 1, g * width : g * width + units]
    cand_ref[...] = total[units + 1 : units + 2, :units]
    loss_ref[...] = total[units + 1 : units + 2, width : width + 128]


def outputs(units, mp, dp, where_dp, plan, blocks):
    rows, cols = blocks[0].shape
    grad = jax.ShapeDtypeStruct((3, mp * units, units), F32)
    return pl.pallas_call(
        functools.partial(output_kernel, units, plan, rows),
        in_specs=[IN_SMEM] + [ANYWHERE] * len(blocks),
        out_specs=[IN_VMEM] * 5,
        out_shape=[
            grad,
            grad,
            jax.ShapeDtypeStruct((3, units), F32),
            jax.ShapeDtypeStruct((1, units), F32),
            jax.ShapeDtypeStruct((1, 128), F32),
        ],
        scratch_shapes=[pltpu.VMEM((rows * dp, cols), F32), pltpu.SemaphoreType.DMA((len(blocks),))],
        compiler_params=pltpu.CompilerParams(vmem_limit_bytes=48 * MIB),
        cost_estimate=pl.CostEstimate(
            flops=0, bytes_accessed=8 * rows * dp * cols, transcendentals=0
        ),
    )(where_dp, *blocks)


def swap(value, k, axis):
    count = lax.axis_size(axis)
    return lax.ppermute(value, axis, [(i, i ^ k) for i in range(count)])


def gather_mp(value):
    count = lax.axis_size("mp")
    if count != 4:
        return [value] + [swap(value, k, "mp") for k in range(1, count)]
    near = swap(value, 1, "mp")
    middle = lax.ppermute(value, "mp", [(1, 2), (2, 1)])
    over = swap(value, 2, "mp")
    far = lax.ppermute(over, "mp", [(1, 0), (2, 3)])
    place_now = lax.axis_index("mp")
    inside = (place_now == 1) | (place_now == 2)
    return [value, near, over, jnp.where(inside, middle, far)]


def after(value, *others):
    return lax.optimization_barrier((value, *others))[0]


def gather_dp(value):
    count = lax.axis_size("dp")
    rows = value.shape[0]
    if count != 8 or rows % 32:
        plan = [(k, 0) for k in range(0, count, 2)]
        pieces = [value] + [swap(value, k, "dp") for k in range(2, count, 2)]
    else:
        half = rows // 2
        one, two = swap(value, 2, "dp"), swap(value, 4, "dp")
        far_one, far_two = swap(two[:half], 2, "dp"), swap(one[half:], 4, "dp")
        plan = [(0, 0), (2, 0), (4, 0), (6, 0), (6, half)]
        pieces = [value, one, two, far_one, far_two]
    other = [swap(piece, 1, "dp") for piece in pieces]
    return tuple(plan + [(k + 1, row) for k, row in plan]), pieces + other


def reduce_dp(kept, sent):
    mine = kept + swap(sent, 1, "dp")
    if mine.shape[0] != 4:
        total = mine[0]
        for k in range(1, mine.shape[0]):
            total = total + swap(mine[k], 2 * k, "dp")
        return total
    half = mine.shape[1] // 2
    one = swap(mine[3, :half], 2, "dp")
    two = swap(mine[3, half:], 4, "dp")
    to_one = jnp.concatenate([mine[1, :half], mine[1, half:] + two])
    to_two = jnp.concatenate([mine[2, :half] + one, mine[2, half:]])
    return mine[0] + swap(to_one, 2, "dp") + swap(to_two, 4, "dp")


def low(value):
    return lax.reduce_precision(value, 8, 7).astype(BF)


def on_device(
    item_ids,
    session_ends,
    negatives,
    embedding,
    in_weight,
    hid_weight,
    gate_bias,
    cand_bias,
    out_table,
    out_bias,
):
    dp, mp = lax.axis_size("dp"), lax.axis_size("mp")
    me_dp, me_mp = lax.axis_index("dp"), lax.axis_index("mp")
    order_dp = me_dp ^ jnp.arange(dp, dtype=jnp.int32)
    order_mp = me_mp ^ jnp.arange(mp, dtype=jnp.int32)
    me = me_mp.astype(jnp.int32).reshape(1)
    steps, slots = session_ends.shape
    events = steps * slots
    feats, vocab = embedding.shape
    units = hid_weight.shape[2]
    width = up(units, 128)
    full = mp * width
    neg_count = negatives.shape[0]
    neg_share = neg_count // dp

    end_float = session_ends.astype(F32)
    keep = jnp.concatenate([jnp.zeros((1, slots), F32), 1.0 - end_float[:-1]], axis=0)
    weight = ((1.0 - end_float) / (steps * slots * dp)).reshape(events, 1)
    sources = item_ids[:-1].reshape(events)
    targets = item_ids[1:].reshape(events)
    own_negs = lax.dynamic_slice_in_dim(negatives, me_dp * neg_share, neg_share)

    def padded_rows(value):
        value = value.reshape(3, mp, units, units)
        value = jnp.pad(value, ((0, 0), (0, 0), (0, width - units), (0, width - units)))
        return value.reshape(3 * full, width)

    share = 3 * full // dp
    in_share = lax.dynamic_slice_in_dim(padded_rows(in_weight), me_dp * share, share)
    hid_share = lax.dynamic_slice_in_dim(padded_rows(hid_weight), me_dp * share, share)
    biases = jnp.pad(
        jnp.concatenate([gate_bias, cand_bias[None]]), ((0, 0), (0, width - units))
    )
    first = low(biases)
    second = low(biases - first.astype(F32))
    third = low(biases - first.astype(F32) - second.astype(F32))
    bias_rows = jnp.concatenate([first, second, third, jnp.zeros((4, width), BF)])
    cols = gather_mp(jnp.concatenate([in_share, hid_share, bias_rows]))
    bias_all = place(cols, order_mp, 1, 2 * share, 16)[:12].astype(F32)
    bias_all = jnp.pad(bias_all[0:4] + bias_all[4:8] + bias_all[8:12], ((0, 4), (0, 0)))
    w_plan, w_blocks = gather_dp(place(cols, order_mp, 1, 0, 2 * share))

    x_rows, x_sid, x_order = lookup([sources], embedding)
    x_pieces = gather_mp(x_rows)
    t_rows, n_rows, t_sid, t_order = lookup([after(targets, cols[-1]), own_negs], out_table, out_bias)
    n_pieces = gather_mp(n_rows)
    t_pieces = gather_mp(after(t_rows, n_pieces[2]))
    n_plan, n_blocks = gather_dp(place(n_pieces, order_mp, 1))
    gap = ((0, 0), (0, t_sid.shape[1] - x_sid.shape[1]))
    lists = jnp.concatenate([jnp.pad(x_sid, gap), jnp.pad(x_order, gap), t_sid, t_order])
    lists = [swap(lists.astype(jnp.int32), k, "dp") if k else lists.astype(jnp.int32) for k in range(dp)]
    lists = jnp.stack(lists)
    x_lists = lists[:, 0:2, : x_sid.shape[1]]
    t_lists = lists[:, 2:4]

    keep = keep[:, :, None]
    z, r, c, inner, prev, hs, own_shown, in_own = forward(
        steps, slots, width, me, order_mp, order_dp, keep, bias_all, x_pieces, w_plan, share, w_blocks
    )
    shown = hs.reshape(events, full)
    own_shown = own_shown.reshape(events, width)
    row_plan, row_blocks = gather_dp(own_shown)
    col = jnp.arange(full)[None, :]
    one_row = ((col >= units) & (col < units + 3)).astype(BF)
    dhs, tgt_low, loss, kept, sent = scores(
        slots, dp, order_mp, shown, own_shown, one_row, weight, t_pieces, n_plan, n_blocks
    )
    neg_sum = reduce_dp(kept, sent).T
    scale_rows = up(-(-events // width), 32)
    scale = jnp.pad(tgt_low.reshape(events), (0, scale_rows * width - events))
    neg_plan, neg_blocks = gather_dp(jnp.concatenate([neg_sum, scale.reshape(scale_rows, width)]))

    dx, own, sums = backward(
        width, me, order_dp, z, r, c, inner, prev, keep, dhs, bias_all, in_own, w_plan, share, w_blocks
    )
    dx_plan, dx_blocks = gather_dp(dx)
    kept, sent = weight_grads(units, order_dp, order_mp, hs, keep, own, sums, loss, x_pieces)
    grad_plan, grad_blocks = gather_dp(reduce_dp(kept, sent))
    in_sum, hid_sum, gate_sum, cand_sum, loss_sum = outputs(
        units, mp, dp, order_dp, grad_plan, grad_blocks
    )

    items = vocab // dp
    base = (me_dp * items).astype(jnp.int32)
    neg_parts = {k: [v for (j, _), v in zip(neg_plan, neg_blocks) if j == k] for k in range(dp)}
    neg_whole = [v[0] if len(v) == 1 else jnp.concatenate(v) for v in neg_parts.values()]
    scale_all = jnp.stack([v[neg_share:].reshape(-1)[:events] for v in neg_whole])
    scale_all = jnp.concatenate([scale_all, jnp.ones((dp, neg_share), F32)], axis=1)
    table_sum, bias_sum = scatter(
        base,
        units,
        items,
        t_lists,
        events,
        row_plan,
        row_blocks,
        scale_all,
        neg_share,
        tuple((k, 0) for k in range(dp)),
        neg_whole,
    )
    (embed_sum,) = scatter(base, units, items, x_lists, events, dx_plan, dx_blocks)
    return (
        loss_sum[0, 0],
        in_sum,
        hid_sum,
        gate_sum,
        cand_sum.reshape(units),
        embed_sum,
        table_sum,
        bias_sum.reshape(items),
    )


def solution(mesh):
    return jax.shard_map(
        on_device,
        mesh=mesh,
        in_specs=(
            P(None, "dp"),
            P(None, "dp"),
            P(),
            P("mp", None),
            P(None, None, "mp"),
            P(None, None, "mp"),
            P(None, "mp"),
            P("mp"),
            P("mp", None),
            P(),
        ),
        out_specs=(
            P(),
            P(None, None, "mp"),
            P(None, None, "mp"),
            P(None, "mp"),
            P("mp"),
            P("mp", "dp"),
            P("mp", "dp"),
            P("dp"),
        ),
        check_vma=False,
    )
```

```python
import functools
import math

import jax
import jax.numpy as jnp
from jax import lax
from jax.experimental import pallas as pl
from jax.experimental.pallas import tpu as pltpu
from jax.sharding import PartitionSpec as P

bpr_weight = 1.0
BF = jnp.bfloat16
F32 = jnp.float32
ITEM_BLOCK = 4096
CHUNK = 256
SCORE_ROWS = 64
UNROLL = 4
GATES_IN = (0, 1, 2)
MIB = 1024 * 1024
ANYWHERE = pl.BlockSpec(memory_space=pl.ANY)
IN_SMEM = pl.BlockSpec(memory_space=pltpu.SMEM)
IN_VMEM = pl.BlockSpec(memory_space=pltpu.VMEM)


def up(count, unit):
    return -(-count // unit) * unit


def lookup_kernel(has_bias, feats, cnt_ref, idr_ref, idc_ref, tab_ref, *rest):
    rest = list(rest)
    bias_ref = rest.pop(0) if has_bias else None
    sid, order, perm, xs, held, sems = rest[-6:]
    outs = rest[:-6]
    count = idr_ref.shape[1]
    blocks, _, width = held.shape

    def fetch(b):
        return pltpu.make_async_copy(
            tab_ref.at[:, pl.ds(b * width, width)], held.at[b], sems.at[b]
        )

    for b in range(blocks):
        fetch(b).start()
    lane = lax.broadcasted_iota(jnp.int32, (CHUNK, count), 1)
    keyr = idr_ref[...] * 4096 + lax.broadcasted_iota(jnp.int32, (1, count), 1)
    sid[...] = jnp.zeros_like(sid)
    order[...] = jnp.zeros_like(order)

    def sort_rows(i, _):
        rows = pl.ds(pl.multiple_of(i * CHUNK, CHUNK), CHUNK)
        idc = idc_ref[rows, :]
        at = i * CHUNK + lax.broadcasted_iota(jnp.int32, (CHUNK, 1), 0)
        keyc = idc * 4096 + at
        rank = jnp.sum((keyr < keyc).astype(F32), axis=1, keepdims=True).astype(jnp.int32)
        hit = rank == lane
        perm[rows, :] = hit.astype(F32).astype(BF)
        sid[...] += jnp.sum(jnp.where(hit, idc, 0).astype(F32), axis=0, keepdims=True)
        order[...] += jnp.sum(jnp.where(hit, at, 0).astype(F32), axis=0, keepdims=True)
        return 0

    lax.fori_loop(0, count // CHUNK, sort_rows, 0)
    xs[...] = jnp.zeros_like(xs)
    for b in range(blocks):
        fetch(b).wait()
        base = b * width

        def pick_chunk(c, _, b=b, base=base):
            cols = pl.ds(pl.multiple_of(c * CHUNK, CHUNK), CHUNK)
            ids = sid[:, cols].astype(jnp.int32) - base
            pick = (lax.broadcasted_iota(jnp.int32, (width, CHUNK), 0) == ids).astype(F32).astype(BF)
            xs[0:feats, cols] += jnp.dot(held[b], pick, preferred_element_type=F32)
            return 0

        lax.fori_loop(
            cnt_ref[b] // CHUNK, (cnt_ref[b + 1] + CHUNK - 1) // CHUNK, pick_chunk, 0
        )
    out = lax.dot_general(
        perm[...], xs[...].astype(BF), (((1,), (1,)), ((), ())), preferred_element_type=F32
    )
    if has_bias:
        value = bias_ref[...]
        first = value.astype(BF).astype(F32)
        second = (value - first).astype(BF).astype(F32)
        parts = (first, second, value - first - second)
        groups = value.shape[0]
        idc = idc_ref[...]
        group = (idc // 128 == lax.broadcasted_iota(jnp.int32, (count, groups), 1)).astype(F32).astype(BF)
        member = lax.broadcasted_iota(jnp.int32, (count, 128), 1) == idc % 128
        col = lax.broadcasted_iota(jnp.int32, out.shape, 1)
        for k, part in enumerate(parts):
            near = jnp.dot(group, part.astype(BF), preferred_element_type=F32)
            own = jnp.sum(jnp.where(member, near, 0.0), axis=1, keepdims=True)
            out = jnp.where(col == feats + k, own, out)
    at = 0
    for ref in outs:
        ref[...] = out[at : at + ref.shape[0]].astype(BF)
        at += ref.shape[0]


def lookup(parts, table, bias=None):
    ids = jnp.concatenate(parts)
    feats, vocab = table.shape
    width = up(feats, 128)
    count = ids.shape[0]
    padded = up(count, CHUNK)
    ids = jnp.concatenate([ids, jnp.full((padded - count,), vocab, jnp.int32)])
    blocks = vocab // ITEM_BLOCK
    edges = jnp.arange(blocks + 1, dtype=jnp.int32) * ITEM_BLOCK
    cnt = jnp.sum((ids[None, :] < edges[:, None]).astype(jnp.int32), axis=1)
    vmem = pl.BlockSpec(memory_space=pltpu.VMEM)
    in_specs = [pl.BlockSpec(memory_space=pltpu.SMEM), vmem, vmem, pl.BlockSpec(memory_space=pl.ANY)]
    args = [cnt, ids.reshape(1, padded), ids.reshape(padded, 1), table]
    if bias is not None:
        in_specs.append(vmem)
        args.append(bias.reshape(vocab // 128, 128))
    return pl.pallas_call(
        functools.partial(lookup_kernel, bias is not None, feats),
        in_specs=in_specs,
        out_specs=[vmem] * (len(parts) + 2),
        scratch_shapes=[
            pltpu.VMEM((padded, padded), BF),
            pltpu.VMEM((width, padded), F32),
            pltpu.VMEM((blocks, feats, ITEM_BLOCK), BF),
            pltpu.SemaphoreType.DMA((blocks,)),
        ],
        out_shape=[
            *[jax.ShapeDtypeStruct((part.shape[0], width), BF) for part in parts],
            jax.ShapeDtypeStruct((1, padded), F32),
            jax.ShapeDtypeStruct((1, padded), F32),
        ],
        compiler_params=pltpu.CompilerParams(vmem_limit_bytes=56 * MIB),
        cost_estimate=pl.CostEstimate(
            flops=2 * vocab * feats * 512, bytes_accessed=vocab * feats * 2, transcendentals=0
        ),
    )(*args)


def scatter_kernel(feats, sources, plan, neg_plan, edge_ref, list_ref, *refs):
    refs = list(refs)
    scaled = neg_plan is not None
    blocks = [refs.pop(0) for _ in plan]
    negs = [refs.pop(0) for _ in neg_plan or ()]
    out_ref = refs.pop(0)
    bias_ref = refs.pop(0) if scaled else None
    total, held, low_rows, low_negs, sems = refs
    items, width = out_ref.shape[1], total.shape[1]
    each = held.shape[0] // sources
    depth = low_rows.shape[0] // sources
    copies = block_copies(plan, depth, blocks, None, low_rows, sems, 0)
    if scaled:
        share, neg_depth = each - depth, low_negs.shape[0] // sources
        copies += block_copies(neg_plan, neg_depth, negs, None, low_negs, sems, len(plan))
    start(copies)
    total[...] = jnp.zeros_like(total)

    def widen(s):
        group = width // 2
        if scaled:
            negs_now = decoded(low_negs[s * neg_depth : (s + 1) * neg_depth, :])
            held[s * each + depth : (s + 1) * each, :] = negs_now[:share]
            scale = negs_now[share:].T
        for at in range(0, depth, group):
            rows = min(group, depth - at)
            wide = low_rows[s * depth + at : s * depth + at + rows, :]
            if scaled:
                col = lax.broadcasted_iota(jnp.int32, wide.shape, 1)
                wide = jnp.where(col == feats, 1.0, wide.astype(F32))
                wide = wide * scale[:rows, at // group : at // group + 1]
            else:
                wide = decoded(wide)
            held[s * each + at : s * each + at + rows, :] = wide

    size = list_ref.shape[0] // edge_ref.shape[0]
    for s in range(sources):
        first, last = edge_ref[s, 0], edge_ref[s, 1]
        for copy, (k, _) in zip(copies, list(plan) + list(neg_plan or ())):
            if k == s:
                copy.wait()
        widen(s)

        begin = s * size + first

        def add(j, carry, begin=begin):
            item, value = carry
            found = []
            for n in range(UNROLL):
                at = begin + j * UNROLL + n
                both = list_ref[at]
                new = both >> 16
                row = both & 65535
                term = held[pl.ds(row, 1), :]
                found.append((new, term, total[pl.ds(new, 1), :]))
            for new, term, ahead in found:
                total[pl.ds(item, 1), :] = value
                value = jnp.where(new == item, value, ahead) + term
                item = new
            return item, value

        turns = (last - first + UNROLL - 1) // UNROLL
        item, value = lax.fori_loop(0, turns, add, (jnp.int32(items), jnp.zeros((1, width), F32)))
        total[pl.ds(item, 1), :] = value

    tile = 512 if items % 512 == 0 else 128
    for at in range(0, items, tile):
        turned = total[at : at + tile, :].T
        out_ref[:, at : at + tile] = turned[:feats]
        if scaled:
            bias_ref[:, at : at + tile] = turned[feats : feats + 1]


def scatter_lists(base, items, ids, rows, each):
    ends = jnp.stack([base, base + items])
    edges = jnp.sum((ids[:, None, :] < ends[None, :, None]).astype(jnp.int32), axis=2)
    gap = ((0, 0), (0, UNROLL))
    own = (ids >= base) & (ids < base + items)
    places = jnp.pad(jnp.where(own, ids - base, items), gap, constant_values=items)
    rows = rows + each * jnp.arange(ids.shape[0])[:, None]
    rows = jnp.pad(jnp.where(own, rows, 0), gap)
    return edges, (places * 65536 + rows).reshape(-1)


def scatter(feats, items, lists, depth, plan, blocks, neg_share=0, neg_plan=None, negs=()):
    width = blocks[0].shape[-1]
    sources = lists[0].shape[0]
    each = depth + neg_share
    edges, lists = lists
    scaled = neg_plan is not None
    out_shape = [jax.ShapeDtypeStruct((feats, items), F32)]
    scratch = [
        pltpu.VMEM((items + 8, width), F32),
        pltpu.VMEM((sources * each, width), F32),
        pltpu.VMEM((sources * depth, width), blocks[0].dtype),
        pltpu.VMEM((sources * negs[0].shape[0] if scaled else 16, width), jnp.int16),
        pltpu.SemaphoreType.DMA((len(blocks) + len(negs),)),
    ]
    if scaled:
        out_shape.append(jax.ShapeDtypeStruct((1, items), F32))
    return pl.pallas_call(
        functools.partial(scatter_kernel, feats, sources, plan, neg_plan),
        in_specs=[IN_SMEM] * 2 + [ANYWHERE] * (len(blocks) + len(negs)),
        out_specs=[IN_VMEM] * len(out_shape),
        out_shape=out_shape,
        scratch_shapes=scratch,
        compiler_params=pltpu.CompilerParams(vmem_limit_bytes=56 * MIB),
        cost_estimate=pl.CostEstimate(
            flops=0, bytes_accessed=sources * each * width * 8, transcendentals=0
        ),
    )(edges, lists, *blocks, *negs)


def place_kernel(first, axis, where_ref, *refs):
    *pieces, out_ref, sems = refs
    size = out_ref.shape[axis] // len(pieces)
    copies = []
    for k, piece in enumerate(pieces):
        spot = pl.ds(pl.multiple_of(where_ref[k] * size, size), size)
        target = out_ref.at[spot, :] if axis == 0 else out_ref.at[:, spot]
        source = piece.at[pl.ds(first, target.shape[0]), :]
        copies.append(pltpu.make_async_copy(source, target, sems.at[k]))
    for copy in copies:
        copy.start()
    for copy in copies:
        copy.wait()


def place(pieces, where, axis, first=0, rows=None):
    shape = [rows or pieces[0].shape[0], pieces[0].shape[1]]
    shape[axis] *= len(pieces)
    anywhere = pl.BlockSpec(memory_space=pl.ANY)
    return pl.pallas_call(
        functools.partial(place_kernel, first, axis),
        in_specs=[pl.BlockSpec(memory_space=pltpu.SMEM)] + [anywhere] * len(pieces),
        out_specs=pl.BlockSpec(memory_space=pltpu.VMEM),
        scratch_shapes=[pltpu.SemaphoreType.DMA((len(pieces),))],
        out_shape=jax.ShapeDtypeStruct(tuple(shape), pieces[0].dtype),
        compiler_params=pltpu.CompilerParams(vmem_limit_bytes=16 * MIB),
        cost_estimate=pl.CostEstimate(
            flops=0, bytes_accessed=4 * shape[0] * shape[1], transcendentals=0
        ),
    )(where, *pieces)


def block_copies(plan, depth, blocks, where_ref, target, sems, first_sem, window=None):
    copies = []
    for i, (block, (k, row)) in enumerate(zip(blocks, plan)):
        size = min(block.shape[0], depth - row) if window is None else window[1]
        first = 0 if window is None else window[0]
        source = block.at[pl.ds(first, size), :]
        unit = math.gcd(depth, row) if row else depth
        at = pl.multiple_of(where_ref[k] * depth + row, unit) if where_ref is not None else k * depth + row
        copies.append(
            pltpu.make_async_copy(source, target.at[pl.ds(at, size), :], sems.at[first_sem + i])
        )
    return copies


def col_copies(pieces, where_ref, target, sems, first_sem):
    rows = target.shape[0]
    copies = []
    for k, piece in enumerate(pieces):
        size = piece.shape[1]
        spot = pl.ds(pl.multiple_of(where_ref[k] * size, size), size)
        copies.append(
            pltpu.make_async_copy(piece.at[pl.ds(0, rows), :], target.at[:, spot], sems.at[first_sem + k])
        )
    return copies


def start(copies):
    for copy in copies:
        copy.start()


def finish(copies):
    for copy in copies:
        copy.wait()


def forward_kernel(mp, plan, share, me_ref, where_mp, where_dp, keep_ref, bias_ref, *refs):
    count = len(plan)
    x_pieces, own_weights, refs = refs[:mp], refs[mp : mp + 2], refs[mp + 2 :]
    blocks = refs[:count]
    z_ref, r_ref, c_ref, q_ref, prev_ref, hs_ref, own_ref, in_own_ref = refs[count : count + 8]
    x_all, in_all, hid_all, state, low_state, acc, from_state, sems = refs[count + 8 :]
    t, q = pl.program_id(0), pl.program_id(1)
    slots, width = z_ref.shape[2:]
    cols = pl.ds(pl.multiple_of(q * width, width), width)
    gates = pl.ds(pl.multiple_of(q * 3 * width, 3 * width), 3 * width)
    x_in = col_copies(x_pieces, where_mp, x_all, sems, 0)
    in_in, hid_in = weight_copies(
        plan, share, own_weights, blocks, where_mp, where_dp, in_all, hid_all, sems, mp
    )

    @pl.when((t == 0) & (q == 0))
    def _():
        start(x_in)
        start(in_in)
        state[...] = jnp.zeros_like(state)
        from_state[...] = jnp.zeros_like(from_state)
        finish(x_in)
        finish(in_in)
        start(hid_in)
        in_own_ref[...] = in_all[pl.ds(pl.multiple_of(me_ref[0] * width, width), width), :]

    @pl.when((t == 1) & (q == 0))
    def _():
        finish(hid_in)

    @pl.when(q == 0)
    def _():
        low_state[...] = (state[...] * keep_ref[0]).astype(BF)

    x = x_all[pl.ds(pl.multiple_of(t * slots, slots), slots), :]
    acc[...] = jnp.dot(x, in_all[:, gates], preferred_element_type=F32) + bias_ref[0:1, :]

    @pl.when(t > 0)
    def _():
        from_state[...] = jnp.dot(low_state[...], hid_all[:, gates], preferred_element_type=F32)

    prev = state[:, cols] * keep_ref[0]
    z = 1.0 / (1.0 + jnp.exp(-(acc[:, :width] + from_state[:, :width])))
    r = 1.0 / (1.0 + jnp.exp(-(acc[:, width : 2 * width] + from_state[:, width : 2 * width])))
    inner = from_state[:, 2 * width :] + bias_ref[1:2, :width]
    c = jnp.tanh(acc[:, 2 * width :] + r * inner)
    h = (1.0 - z) * prev + z * c
    z_ref[0, 0] = z
    r_ref[0, 0] = r
    c_ref[0, 0] = c
    q_ref[0, 0] = inner
    prev_ref[0, 0] = prev
    shown = h.astype(BF)
    hs_ref[0] = shown
    state[:, cols] = h

    @pl.when(q == me_ref[0])
    def _():
        own_ref[0] = shown


def weight_copies(plan, share, own, blocks, where_mp, where_dp, in_all, hid_all, sems, first_sem):
    made = []
    for part, target in enumerate((in_all, hid_all)):
        made.append([])
        if target is None:
            continue
        gates = own[part].shape[1]
        sem = sems.at[first_sem + part]

        def copy(source, rows, k, part=part, target=target, gates=gates, sem=sem):
            cols = pl.ds(pl.multiple_of(where_mp[k] * gates, gates), gates)
            made[part].append(pltpu.make_async_copy(source, target.at[rows, cols], sem))

        copy(own[part], slice(None), 0)
        for block, (k, row) in zip(blocks, plan):
            if not row <= part * share < row + block.shape[0]:
                continue
            rows = pl.ds(pl.multiple_of(where_dp[k] * share, share), share)
            for j in range(block.shape[1] // gates):
                source = block.at[pl.ds(part * share - row, share), pl.ds(j * gates, gates)]
                copy(source, rows, j + 1)
    return made


def forward(
    steps, slots, width, me, where_mp, where_dp, keep, bias_all, x_pieces, own_weights, plan, share, blocks
):
    mp, count = len(x_pieces), len(blocks)
    full = mp * width
    tile = pl.BlockSpec((1, 1, slots, width), lambda t, q: (t, q, 0, 0))
    later = pl.BlockSpec(
        (1, 1, slots, width), lambda t, q: (jnp.maximum(t - 1, 0), jnp.where(t == 0, 0, q), 0, 0)
    )
    shape = lambda n: jax.ShapeDtypeStruct((n, mp, slots, width), F32)
    return pl.pallas_call(
        functools.partial(forward_kernel, mp, plan, share),
        grid=(steps, mp),
        in_specs=[IN_SMEM] * 3
        + [
            pl.BlockSpec((1, slots, 1), lambda t, q: (t, 0, 0)),
            pl.BlockSpec((8, 3 * width), lambda t, q: (0, q)),
        ]
        + [ANYWHERE] * (mp + 2 + count),
        out_specs=[
            tile,
            tile,
            tile,
            later,
            later,
            pl.BlockSpec((1, slots, width), lambda t, q: (t, 0, q)),
            pl.BlockSpec((1, slots, width), lambda t, q: (t, 0, 0)),
            pl.BlockSpec((width, 3 * full), lambda t, q: (0, 0)),
        ],
        out_shape=[shape(steps)] * 3
        + [shape(steps - 1)] * 2
        + [
            jax.ShapeDtypeStruct((steps, slots, full), BF),
            jax.ShapeDtypeStruct((steps, slots, width), BF),
            jax.ShapeDtypeStruct((width, 3 * full), BF),
        ],
        scratch_shapes=[
            pltpu.VMEM((steps * slots, full), BF),
            pltpu.VMEM((full, 3 * full), BF),
            pltpu.VMEM((full, 3 * full), BF),
            pltpu.VMEM((slots, full), F32),
            pltpu.VMEM((slots, full), BF),
            pltpu.VMEM((slots, 3 * width), F32),
            pltpu.VMEM((slots, 3 * width), F32),
            pltpu.SemaphoreType.DMA((mp + 2,)),
        ],
        compiler_params=pltpu.CompilerParams(vmem_limit_bytes=48 * MIB),
        cost_estimate=pl.CostEstimate(
            flops=2 * 6 * steps * slots * full * full,
            bytes_accessed=steps * full * (slots * 24 + full * 12),
            transcendentals=3 * steps * slots * full,
        ),
    )(me, where_mp, where_dp, keep, bias_all, *x_pieces, *own_weights, *blocks)


def score_kernel(rows, mp, plan, dp, where_mp, hs_ref, own_ref, one_ref, weight_ref, *refs):
    count = len(plan)
    tgt_pieces, blocks = refs[:mp], refs[mp : mp + count]
    ds_ref, dhs_ref, du_ref, loss_ref, kept_ref, sent_ref, s_ref, tgt_all, neg_all, table, sems = refs[mp + count :]
    i = pl.program_id(0)
    tile = hs_ref.shape[0]
    share, width = kept_ref.shape[1:]
    tgt_in = col_copies(tgt_pieces, where_mp, tgt_all, sems, 0)
    neg_in = block_copies(plan, share, blocks, None, neg_all, sems, mp)

    @pl.when(i == 0)
    def _():
        start(neg_in)
        start(tgt_in)
        loss_ref[...] = jnp.zeros_like(loss_ref)
        table[...] = jnp.zeros_like(table)
        finish(neg_in)

    s_ref[...] = lax.dot_general(
        hs_ref[...] + one_ref[...], neg_all[...], (((1,), (1,)), ((), ())), preferred_element_type=F32
    )

    @pl.when(i == 0)
    def _():
        finish(tgt_in)

    def chunk(j, _):
        at = pl.ds(pl.multiple_of(j * rows, rows), rows)
        s = s_ref[at, :]
        w = weight_ref[at, :]
        tgt = tgt_all[pl.ds(pl.multiple_of(i * tile + j * rows, rows), rows), :].astype(F32)
        u = jnp.sum((hs_ref[at, :] + one_ref[...]).astype(F32) * tgt, axis=1, keepdims=True)
        top = jnp.max(s, axis=1, keepdims=True)
        e = jnp.exp(s - top)
        above = 1.0 / (1.0 + jnp.exp(s - u))
        ea = e * above
        inv = 1.0 / jnp.sum(e, axis=1, keepdims=True)
        mixture = jnp.sum(ea, axis=1, keepdims=True) * inv
        spread = jnp.sum(e * s * s, axis=1, keepdims=True) * inv
        slope = jnp.sum(ea * (1.0 - above), axis=1, keepdims=True) * inv
        shift = s + 1.0
        ds = (w * inv * e) * (bpr_weight * (shift * shift - spread) - above * above * (1.0 / mixture))
        ds_ref[at, :] = ds.astype(BF)
        du_ref[at, :] = (-w * slope / mixture).astype(BF).astype(F32)
        loss_ref[...] += jnp.broadcast_to(
            jnp.sum(w * (-jnp.log(mixture) + bpr_weight * spread), keepdims=True), loss_ref.shape
        )
        return 0

    lax.fori_loop(0, tile // rows, chunk, 0)
    own = pl.ds(pl.multiple_of(i * tile, tile), tile)
    dhs = jnp.dot(ds_ref[...], neg_all[...], preferred_element_type=F32)
    dhs += du_ref[...] * tgt_all[own, :].astype(F32)
    for q in range(mp):
        dhs_ref[q] = dhs[:, q * width : (q + 1) * width]
    counted = own_ref[...] + one_ref[:, :width]
    table[...] += lax.dot_general(counted, ds_ref[...], (((0,), (0,)), ((), ())), preferred_element_type=F32)

    @pl.when(i == pl.num_programs(0) - 1)
    def _():
        for k in range(dp // 2):
            kept_ref[k] = table[:, 2 * k * share : (2 * k + 1) * share].T
            sent_ref[k] = table[:, (2 * k + 1) * share : (2 * k + 2) * share].T


def scores(tile, dp, where_mp, shown, own_shown, one_row, weight, tgt_pieces, plan, blocks):
    events, full = shown.shape
    width = own_shown.shape[1]
    mp = len(tgt_pieces)
    share = blocks[0].shape[0]
    count = dp * share
    rows = next(n for n in (SCORE_ROWS, 32, 8) if tile % n == 0)
    row_tile = lambda w: pl.BlockSpec((tile, w), lambda i: (i, 0))
    half = jax.ShapeDtypeStruct((dp // 2, share, width), F32)
    half_spec = pl.BlockSpec((dp // 2, share, width), lambda i: (0, 0, 0))
    return pl.pallas_call(
        functools.partial(score_kernel, rows, mp, plan, dp),
        grid=(events // tile,),
        in_specs=[
            IN_SMEM,
            row_tile(full),
            row_tile(width),
            pl.BlockSpec((1, full), lambda i: (0, 0)),
            row_tile(1),
        ]
        + [ANYWHERE] * (mp + len(blocks)),
        out_specs=[
            pl.BlockSpec((tile, count), lambda i: (0, 0)),
            pl.BlockSpec((mp, tile, width), lambda i: (0, i, 0)),
            row_tile(1),
            pl.BlockSpec((8, 128), lambda i: (0, 0)),
            half_spec,
            half_spec,
        ],
        out_shape=[
            jax.ShapeDtypeStruct((tile, count), BF),
            jax.ShapeDtypeStruct((mp, events, width), F32),
            jax.ShapeDtypeStruct((events, 1), F32),
            jax.ShapeDtypeStruct((8, 128), F32),
            half,
            half,
        ],
        scratch_shapes=[
            pltpu.VMEM((tile, count), F32),
            pltpu.VMEM((events, full), BF),
            pltpu.VMEM((count, full), BF),
            pltpu.VMEM((width, count), F32),
            pltpu.SemaphoreType.DMA((mp + len(blocks),)),
        ],
        compiler_params=pltpu.CompilerParams(vmem_limit_bytes=48 * MIB),
        cost_estimate=pl.CostEstimate(
            flops=4 * events * full * count,
            bytes_accessed=events * (full * 8 + count * 2) + count * full * 2,
            transcendentals=3 * events * count,
        ),
    )(where_mp, shown, own_shown, one_row, weight, *tgt_pieces, *blocks)[1:]


def coded(rows, units):
    col = lax.broadcasted_iota(jnp.int32, rows.shape, 1)
    rows = jnp.where(col < units, rows, 0.0)
    top = jnp.max(jnp.abs(rows), axis=1, keepdims=True)
    power = jnp.clip(jnp.ceil(jnp.log2(top)), -90.0, 110.0)
    code = jnp.floor(rows * jnp.exp2(14.0 - power) + 0.5)
    return jnp.where(col == rows.shape[1] - 1, power, code).astype(jnp.int32).astype(jnp.int16)


def decoded(codes):
    wide = codes.astype(jnp.int32).astype(F32)
    return wide * jnp.exp2(wide[:, -1:] - 14.0)


def backward_kernel(
    steps, units, plan, share, me_ref, where_mp, where_dp, z_ref, r_ref, c_ref, q_ref, prev_ref, keep_ref, dhs_ref, bias_ref, in_ref, *refs
):
    count = len(plan)
    own_weights, blocks, refs = (None, refs[0]), refs[1 : 1 + count], refs[1:]
    dx_one, dx_two, own_ref, sum_ref, dx_ref, later, back, hid_all, sems = refs[count:]
    i, q = pl.program_id(0), pl.program_id(1)
    last_step, last_part = steps - 1, pl.num_programs(1) - 1
    width = z_ref.shape[3]
    cols = pl.ds(pl.multiple_of(q * width, width), width)
    gates = pl.ds(pl.multiple_of(q * 3 * width, 3 * width), 3 * width)
    _, hid_in = weight_copies(
        plan, share, own_weights, blocks, where_mp, where_dp, None, hid_all, sems, 0
    )

    @pl.when((i == 0) & (q == 0))
    def _():
        start(hid_in)
        later[...] = jnp.zeros_like(later)
        sum_ref[...] = jnp.zeros_like(sum_ref)

    @pl.when(q == 0)
    def _():
        dx_ref[...] = jnp.zeros_like(dx_ref)
        back[...] = jnp.zeros_like(back)

    z, r, c = z_ref[0, 0], r_ref[0, 0], c_ref[0, 0]
    begun = i < last_step
    inner = jnp.where(begun, q_ref[0, 0], jnp.broadcast_to(bias_ref[1:2, :width], z.shape))
    prev = jnp.where(begun, prev_ref[0, 0], 0.0)
    dh = later[:, cols] + dhs_ref[0]
    rest = 1.0 - z
    dz = dh * (c - prev) * z * rest
    da = dh * z * (1.0 - c * c)
    dr = da * inner * r * (1.0 - r)
    dq = da * r
    grads = (dz, dr, da, dq)
    zl, rl, al, ql = [v.astype(BF) for v in grads]
    over = (((1,), (1,)), ((), ()))
    dx_ref[...] += lax.dot_general(
        jnp.concatenate([zl, rl, al], axis=1), in_ref[...], over, preferred_element_type=F32
    )

    @pl.when((i == 0) & (q == 0))
    def _():
        finish(hid_in)

    @pl.when(begun)
    def _():
        back[...] += lax.dot_general(
            jnp.concatenate([zl, rl, ql], axis=1), hid_all[:, gates], over, preferred_element_type=F32
        )
        back[:, cols] += dh * rest

    @pl.when(q == me_ref[0])
    def _():
        for k, value in enumerate((zl, rl, al, ql)):
            own_ref[:, k * width : (k + 1) * width] = value
            sum_ref[k : k + 1, :] += jnp.sum(grads[k], axis=0, keepdims=True)

    @pl.when(q == last_part)
    def _():
        later[...] = back[...] * keep_ref[0]

    slots, half = dx_ref.shape[0], dx_one.shape[0]
    for t in range(last_step + 1):

        @pl.when((q == last_part) & (i == last_step - t))
        def _(t=t):
            for ref, low, high in ((dx_one, 0, half), (dx_two, half, 2 * half)):
                first, last = max(low, t * slots), min(high, (t + 1) * slots)
                if first < last:
                    ref[first - low : last - low, :] = coded(
                        dx_ref[first - t * slots : last - t * slots, :], units
                    )


def backward(
    units,
    width,
    me,
    where_mp,
    where_dp,
    z,
    r,
    c,
    inner,
    prev,
    keep,
    dhs,
    bias_all,
    in_own,
    own_hid,
    plan,
    share,
    blocks,
):
    steps, parts, slots, _ = z.shape
    full = parts * width
    tile = pl.BlockSpec((1, 1, slots, width), lambda i, q: (steps - 1 - i, q, 0, 0))
    later = pl.BlockSpec(
        (1, 1, slots, width),
        lambda i, q: (jnp.maximum(steps - 2 - i, 0), jnp.where(i == steps - 1, parts - 1, q), 0, 0),
    )
    row = lambda w: pl.BlockSpec((slots, w), lambda i, q: (steps - 1 - i, 0))
    half = steps * slots // 2
    half_spec = pl.BlockSpec((half, width), lambda i, q: (0, 0))
    return pl.pallas_call(
        functools.partial(backward_kernel, steps, units, plan, share),
        grid=(steps, parts),
        in_specs=[IN_SMEM] * 3
        + [tile] * 3
        + [later] * 2
        + [
            pl.BlockSpec((1, slots, 1), lambda i, q: (steps - 1 - i, 0, 0)),
            pl.BlockSpec((1, slots, width), lambda i, q: (q, steps - 1 - i, 0)),
            pl.BlockSpec((8, 3 * width), lambda i, q: (0, q)),
            pl.BlockSpec((width, 3 * width), lambda i, q: (0, q)),
        ]
        + [ANYWHERE] * (1 + len(blocks)),
        out_specs=[half_spec, half_spec, row(4 * width), pl.BlockSpec((8, width), lambda i, q: (0, 0))],
        out_shape=[
            jax.ShapeDtypeStruct((half, width), jnp.int16),
            jax.ShapeDtypeStruct((half, width), jnp.int16),
            jax.ShapeDtypeStruct((steps * slots, 4 * width), BF),
            jax.ShapeDtypeStruct((8, width), F32),
        ],
        scratch_shapes=[
            pltpu.VMEM((slots, width), F32),
            pltpu.VMEM((slots, full), F32),
            pltpu.VMEM((slots, full), F32),
            pltpu.VMEM((full, 3 * full), BF),
            pltpu.SemaphoreType.DMA((2,)),
        ],
        compiler_params=pltpu.CompilerParams(vmem_limit_bytes=48 * MIB),
        cost_estimate=pl.CostEstimate(
            flops=2 * steps * slots * full * (3 * full + 3 * width),
            bytes_accessed=steps * full * (slots * 24 + full * 6),
            transcendentals=0,
        ),
    )(me, where_mp, where_dp, z, r, c, inner, prev, keep, dhs, bias_all, in_own, own_hid, *blocks)


def weights_kernel(units, mp, order_ref, where_mp, hs_ref, keep_ref, own_ref, sum_ref, loss_ref, *refs):
    x_pieces = refs[:mp]
    kept_ref, sent_ref, total, x_all, sems, out_sems = refs[mp:]
    x_in = col_copies(x_pieces, where_mp, x_all, sems, 0)
    start(x_in)
    rows_out = kept_ref.shape[1]

    def blocks_out(part):
        half = total.shape[1] // 2
        cols = slice(part * half, (part + 1) * half)
        copies = []
        for k in range(kept_ref.shape[0]):
            for ref, at in ((kept_ref, 2 * k), (sent_ref, 2 * k + 1)):
                rows = pl.ds(pl.multiple_of(order_ref[at] * rows_out, rows_out), rows_out)
                sem = out_sems.at[part, at]
                copies.append(pltpu.make_async_copy(total.at[rows, cols], ref.at[k, :, cols], sem))
        return copies

    width = sum_ref.shape[1]
    events = x_all.shape[0]
    slots = hs_ref.shape[1]
    over = (((0,), (0,)), ((), ()))
    three = 3 * width
    part = jnp.zeros((total.shape[0], three), F32)
    for t in range(events // slots - 1):
        hb = (hs_ref[t].astype(F32) * keep_ref[t + 1]).astype(BF)
        rows = slice((t + 1) * slots, (t + 2) * slots)
        state = jnp.concatenate([own_ref[rows, : 2 * width], own_ref[rows, three:]], axis=1)
        part += lax.dot_general(hb, state, over, preferred_element_type=F32)
    total[:, three:] = part
    hid_out = blocks_out(1)
    start(hid_out)
    finish(x_in)
    total[:, :three] = lax.dot_general(x_all[...], own_ref[:, :three], over, preferred_element_type=F32)
    for k in range(3):
        total[units : units + 1, k * width : (k + 1) * width] = sum_ref[k : k + 1, :]
    total[units + 1 : units + 2, :width] = sum_ref[3:4, :]
    total[units + 1 : units + 2, width : width + 128] = loss_ref[0:1, :]
    in_out = blocks_out(0)
    start(in_out)
    finish(hid_out)
    finish(in_out)


def weight_grads(units, order, where_mp, hs, keep, own, sums, loss, x_pieces):
    mp = len(x_pieces)
    events, width = own.shape[0], sums.shape[1]
    full = hs.shape[2]
    count = order.shape[0]
    half = jax.ShapeDtypeStruct((count // 2, full // count, 6 * width), F32)
    return pl.pallas_call(
        functools.partial(weights_kernel, units, mp),
        in_specs=[IN_SMEM] * 2 + [IN_VMEM] * 5 + [ANYWHERE] * mp,
        out_specs=[ANYWHERE, ANYWHERE],
        out_shape=[half, half],
        scratch_shapes=[
            pltpu.VMEM((full, 6 * width), F32),
            pltpu.VMEM((events, full), BF),
            pltpu.SemaphoreType.DMA((mp,)),
            pltpu.SemaphoreType.DMA((2, count)),
        ],
        compiler_params=pltpu.CompilerParams(vmem_limit_bytes=56 * MIB),
        cost_estimate=pl.CostEstimate(
            flops=2 * events * full * 6 * width,
            bytes_accessed=events * full * 4 + full * 24 * width,
            transcendentals=0,
        ),
    )(order, where_mp, hs, keep, own, sums, loss, *x_pieces)


def neg_seal_kernel(feats, *refs):
    *terms, scale_ref, out_ref = refs
    total = terms[0][...]
    for term in terms[1:]:
        total += term[...]
    share = total.shape[0]
    out_ref[:share, :] = coded(total, feats)
    out_ref[share:, :] = coded(scale_ref[...], total.shape[1] // 2)


def neg_seal(feats, terms, scale):
    share, width = terms[0].shape
    return pl.pallas_call(
        functools.partial(neg_seal_kernel, feats),
        in_specs=[IN_VMEM] * (len(terms) + 1),
        out_specs=IN_VMEM,
        out_shape=jax.ShapeDtypeStruct((share + scale.shape[0], width), jnp.int16),
        cost_estimate=pl.CostEstimate(
            flops=0, bytes_accessed=4 * len(terms) * share * width, transcendentals=0
        ),
    )(*terms, scale)


def seal_kernel(units, *refs):
    *terms, out_ref = refs
    total = terms[0][...]
    for term in terms[1:]:
        total += term[...]
    width = total.shape[1] // 6
    for k in range(6):
        out_ref[:, k * width : (k + 1) * width] = coded(total[:, k * width : (k + 1) * width], units)


def seal(units, terms):
    return pl.pallas_call(
        functools.partial(seal_kernel, units),
        in_specs=[IN_VMEM] * len(terms),
        out_specs=IN_VMEM,
        out_shape=jax.ShapeDtypeStruct(terms[0].shape, jnp.int16),
        cost_estimate=pl.CostEstimate(
            flops=0, bytes_accessed=4 * len(terms) * terms[0].size, transcendentals=0
        ),
    )(*terms)


def output_kernel(units, plan, depth, where_dp, *refs):
    count = len(plan)
    in_ref, hid_ref, gate_ref, cand_ref, loss_ref, codes, total, sems = refs[count:]
    copies = block_copies(plan, depth, refs[:count], where_dp, codes, sems, 0)
    start(copies)
    finish(copies)
    width = total.shape[1] // 6
    for k in range(6):
        for at in range(0, total.shape[0], width):
            part = (slice(at, at + width), slice(k * width, (k + 1) * width))
            total[part] = decoded(codes[part])
    for k, ref in enumerate((in_ref, hid_ref)):
        for g in range(3):
            at = (3 * k + g) * width
            for q in range(total.shape[0] // width):
                ref[g, q * units : (q + 1) * units, :] = total[q * width : q * width + units, at : at + units]
    for g in range(3):
        gate_ref[g : g + 1, :] = total[units : units + 1, g * width : g * width + units]
    cand_ref[...] = total[units + 1 : units + 2, :units]
    loss_ref[...] = total[units + 1 : units + 2, width : width + 128]


def outputs(units, mp, dp, where_dp, plan, blocks):
    rows, cols = blocks[0].shape
    grad = jax.ShapeDtypeStruct((3, mp * units, units), F32)
    return pl.pallas_call(
        functools.partial(output_kernel, units, plan, rows),
        in_specs=[IN_SMEM] + [ANYWHERE] * len(blocks),
        out_specs=[IN_VMEM] * 5,
        out_shape=[
            grad,
            grad,
            jax.ShapeDtypeStruct((3, units), F32),
            jax.ShapeDtypeStruct((1, units), F32),
            jax.ShapeDtypeStruct((1, 128), F32),
        ],
        scratch_shapes=[
            pltpu.VMEM((rows * dp, cols), jnp.int16),
            pltpu.VMEM((rows * dp, cols), F32),
            pltpu.SemaphoreType.DMA((len(blocks),)),
        ],
        compiler_params=pltpu.CompilerParams(vmem_limit_bytes=48 * MIB),
        cost_estimate=pl.CostEstimate(
            flops=0, bytes_accessed=8 * rows * dp * cols, transcendentals=0
        ),
    )(where_dp, *blocks)


def swap(value, k, axis):
    count = lax.axis_size(axis)
    return lax.ppermute(value, axis, [(i, i ^ k) for i in range(count)])


def after(value, *others):
    return lax.optimization_barrier((value, *others))[0]


def join(*values):
    return lax.optimization_barrier(values)


def mp_near(value):
    count = lax.axis_size("mp")
    if count != 4:
        return [value] + [swap(value, k, "mp") for k in range(1, count)]
    middle = lax.ppermute(value, "mp", [(1, 2), (2, 1)])
    return [value, swap(value, 1, "mp"), swap(value, 2, "mp"), middle]


def mp_far(pieces):
    if lax.axis_size("mp") != 4:
        return pieces
    value, near, over, middle = pieces
    far = lax.ppermute(over, "mp", [(1, 0), (2, 3)])
    me = lax.axis_index("mp")
    return [value, near, over, jnp.where((me == 1) | (me == 2), middle, far)]


def dp_near(value, direct=False):
    count = lax.axis_size("dp")
    if count != 8 or value.shape[0] % 32 or direct:
        return [value] + [swap(value, k, "dp") for k in range(2, count, 2)]
    return [value, swap(value, 2, "dp"), swap(value, 4, "dp")]


def dp_far(pieces):
    count = lax.axis_size("dp")
    if len(pieces) == count // 2:
        return [(k, 0) for k in range(0, count, 2)], pieces
    value, one, two = pieces
    half = value.shape[0] // 2
    far_one, far_two = swap(two[:half], 2, "dp"), swap(one[half:], 4, "dp")
    return [(0, 0), (2, 0), (4, 0), (6, 0), (6, half)], [value, one, two, far_one, far_two]


def dp_near_halves(one, two):
    count = lax.axis_size("dp")
    far = range(2, count, 2) if count != 8 else (2, 4)
    return [[half] + [swap(half, k, "dp") for k in far] for half in (one, two)]


def dp_far_halves(first, second):
    count = lax.axis_size("dp")
    half = first[0].shape[0]
    ways = range(0, count, 2) if count != 8 else (0, 2, 4)
    plan = [(k, row) for row in (0, half) for k in ways]
    pieces = first + second
    if count == 8:
        plan += [(6, 0), (6, half)]
        pieces = pieces + [swap(first[2], 2, "dp"), swap(second[1], 4, "dp")]
    return plan, pieces


def dp_cores(plan, pieces, known=()):
    other = list(known) + [swap(piece, 1, "dp") for piece in pieces[len(known) :]]
    return tuple(plan + [(k + 1, row) for k, row in plan]), pieces + other


def sum_near(mine):
    if mine.shape[0] != 4:
        return mine, [swap(mine[k], 2 * k, "dp") for k in range(1, mine.shape[0])]
    half = mine.shape[1] // 2
    return mine, [swap(mine[3, :half], 2, "dp"), swap(mine[3, half:], 4, "dp")]


def sum_far(mine, got):
    if mine.shape[0] != 4:
        return [mine[0]] + got
    half = mine.shape[1] // 2
    to_one = jnp.concatenate([mine[1, :half], mine[1, half:] + got[1]])
    to_two = jnp.concatenate([mine[2, :half] + got[0], mine[2, half:]])
    return [mine[0], swap(to_one, 2, "dp"), swap(to_two, 4, "dp")]


def low(value):
    return lax.reduce_precision(value, 8, 7).astype(BF)


def on_device(
    item_ids,
    session_ends,
    negatives,
    embedding,
    in_weight,
    hid_weight,
    gate_bias,
    cand_bias,
    out_table,
    out_bias,
):
    dp, mp = lax.axis_size("dp"), lax.axis_size("mp")
    me_dp, me_mp = lax.axis_index("dp"), lax.axis_index("mp")
    order_dp = me_dp ^ jnp.arange(dp, dtype=jnp.int32)
    order_mp = me_mp ^ jnp.arange(mp, dtype=jnp.int32)
    me = me_mp.astype(jnp.int32).reshape(1)
    steps, slots = session_ends.shape
    events = steps * slots
    feats, vocab = embedding.shape
    units = hid_weight.shape[2]
    width = up(units, 128)
    full = mp * width
    neg_count = negatives.shape[0]
    neg_share = neg_count // dp

    end_float = session_ends.astype(F32)
    keep = jnp.concatenate([jnp.zeros((1, slots), F32), 1.0 - end_float[:-1]], axis=0)
    weight = ((1.0 - end_float) / (steps * slots * dp)).reshape(events, 1)
    sources = item_ids[:-1].reshape(events)
    targets = item_ids[1:].reshape(events)
    own_negs = lax.dynamic_slice_in_dim(negatives, me_dp * neg_share, neg_share)

    share = full // dp
    start_row = me_dp * share // width * units + me_dp * share % width

    def row_share(value, gates):
        value = jnp.pad(value, ((0, 0), (0, width - units), (0, 0)))
        value = lax.dynamic_slice(value, (0, start_row, 0), (3, share, units))
        value = jnp.pad(value, ((0, 0), (0, 0), (0, width - units)))
        return jnp.concatenate([value[g] for g in gates], axis=1)

    def own_columns(value, gates):
        value = jnp.pad(value, ((0, 0), (0, width - units), (0, width - units)))
        value = jnp.concatenate([value[:, q * units : q * units + width] for q in range(mp)], axis=1)
        return jnp.concatenate([value[g] for g in gates], axis=1)

    biases = jnp.pad(jnp.concatenate([gate_bias, cand_bias[None]]), ((0, 0), (0, width - units)))
    first = low(biases)
    second = low(biases - first.astype(F32))
    third = low(biases - first.astype(F32) - second.astype(F32))
    bias_rows = [v[:3].reshape(1, 3 * width) for v in (first, second, third)]
    bias_rows.append(jnp.concatenate([first[3], second[3], third[3]]).reshape(1, 3 * width))
    bias_rows = jnp.pad(jnp.concatenate(bias_rows), ((0, 12), (0, 0)))

    w_mine = jnp.concatenate(
        [row_share(in_weight, GATES_IN), row_share(hid_weight, (0, 1, 2)), bias_rows]
    )
    w_cols, x_found = join(mp_near(w_mine), lookup([sources], embedding))
    own_weights = [own_columns(after(in_weight, x_found), GATES_IN), own_columns(after(hid_weight, x_found), (0, 1, 2))]
    w_cols, own_weights = join(mp_far(w_cols), own_weights)
    x_rows, x_sid, x_order = x_found
    w_near = dp_near(jnp.concatenate([v[: 2 * share] for v in w_cols[1:]], axis=1))
    x_near = mp_near(after(x_rows, w_cols))
    bias_all = place(w_cols, order_mp, 1, 2 * share, 16).astype(F32)
    cand_all = jnp.sum(bias_all[3].reshape(mp, 3, width), axis=1)
    cand_all = jnp.pad(cand_all, ((0, 0), (0, 2 * width))).reshape(3 * full)
    bias_all = jnp.pad(jnp.stack([bias_all[0] + bias_all[1] + bias_all[2], cand_all]), ((0, 6), (0, 0)))

    t_found = lookup([after(targets, w_cols), own_negs], out_table, out_bias)
    w_near, x_near, t_found = join(w_near, x_near, t_found)
    t_rows, n_rows, t_sid, t_order = t_found
    n_cols = [n_rows] + [swap(n_rows, k, "mp") for k in range(1, mp)]
    w_plan, w_pieces = dp_far(w_near)
    w_pieces, x_pieces, n_cols = join(w_pieces, mp_far(x_near), n_cols)
    w_plan, w_blocks = dp_cores(w_plan, w_pieces)
    t_near = mp_near(t_rows)
    n_near = dp_near(place(n_cols, order_mp, 1))

    keep = keep[:, :, None]
    made = forward(
        steps,
        slots,
        width,
        me,
        order_mp,
        order_dp,
        keep,
        bias_all,
        x_pieces,
        own_weights,
        w_plan,
        share,
        w_blocks,
    )
    t_near, n_near, made = join(t_near, n_near, made)
    z, r, c, inner, prev, hs, own_shown, in_own = made
    t_pieces = mp_far(t_near)
    n_plan, n_blocks = dp_cores(*dp_far(n_near))
    shown = hs.reshape(events, full)
    own_shown = own_shown.reshape(events, width)
    lists = jnp.concatenate([x_sid, x_order, t_sid, t_order], axis=1).astype(jnp.int32)
    list_size = lists.shape[1]
    block_rows = up(events + up(2 * list_size, width) // width, 64)
    digits = jnp.concatenate([lists // 256, lists % 256], axis=1)
    digits = jnp.pad(digits, ((0, 0), (0, (block_rows - events) * width - 2 * list_size)))
    row_near = dp_near(
        jnp.concatenate([own_shown, digits.astype(BF).reshape(block_rows - events, width)])
    )
    col = jnp.arange(full)[None, :]
    one_row = ((col >= units) & (col < units + 3)).astype(BF)
    scored = scores(
        slots, dp, order_mp, shown, own_shown, one_row, weight, t_pieces, n_plan, n_blocks
    )
    row_near, scored = join(row_near, scored)
    dhs, tgt_low, loss, neg_kept, neg_sent = scored
    row_plan, row_pieces = dp_far(row_near)
    neg_mine = neg_kept + swap(neg_sent, 1, "dp")
    neg_got = [swap(neg_mine[k], 2 * k, "dp") for k in range(1, dp // 2)]

    moved = backward(
        units,
        width,
        me,
        order_mp,
        order_dp,
        z,
        r,
        c,
        inner,
        prev,
        keep,
        dhs,
        bias_all,
        in_own,
        own_weights[1],
        w_plan,
        share,
        w_blocks,
    )
    row_pieces, neg_got, moved = join(row_pieces, neg_got, moved)
    dx_one, dx_two, own, sums = moved
    scale_rows = up(-(-events // (width // 2)), 16)
    scale = jnp.pad(tgt_low.reshape(events), (0, scale_rows * (width // 2) - events), constant_values=1.0)
    scale = jnp.pad(scale.reshape(scale_rows, width // 2), ((0, 0), (0, width - width // 2)))
    neg_block = neg_seal(units + 1, [neg_mine[0]] + neg_got, scale)
    neg_near = dp_near(neg_block, True)
    weighed = weight_grads(units, after(order_dp, neg_block), order_mp, hs, keep, own, sums, loss, x_pieces)
    one_near, two_near = dp_near_halves(dx_one, after(dx_two, weighed))
    one_near, neg_near, weighed = join(one_near, neg_near, weighed)
    grad_kept, grad_sent = weighed
    grad_mine = grad_kept + swap(grad_sent, 1, "dp")
    neg_plan, neg_pieces = dp_far(neg_near)
    neg_plan, neg_blocks = dp_cores(neg_plan, after(neg_pieces, grad_mine))
    row_plan, row_blocks = dp_cores(row_plan, after(row_pieces, grad_mine))
    grad_mine, grad_got = sum_near(grad_mine)
    grad_got, row_blocks, neg_blocks, two_near = join(grad_got, row_blocks, neg_blocks, two_near)
    grad_terms = sum_far(grad_mine, grad_got)
    dx_plan, dx_pieces = dp_far_halves(one_near, two_near)
    lists = []
    for k in range(dp):
        found = []
        for (j, row), v in zip(row_plan, row_blocks):
            if j == k and row + v.shape[0] > events:
                found.append(v[max(events - row, 0) :])
        lists.append(jnp.concatenate(found).reshape(-1)[: 2 * list_size])
    lists = jnp.stack(lists).astype(jnp.int32)
    lists = lists[:, :list_size] * 256 + lists[:, list_size:]
    ends = [0, x_sid.shape[1], 2 * x_sid.shape[1], list_size - t_sid.shape[1], list_size]
    x_ids, x_at, t_ids, t_at = [lists[:, i:j] for i, j in zip(ends, ends[1:])]
    items = vocab // dp
    base = (me_dp * items).astype(jnp.int32)
    x_lists = scatter_lists(base, items, x_ids, x_at, events)
    t_lists = scatter_lists(base, items, t_ids, t_at, events + neg_share)
    tabled = scatter(
        units, items, t_lists, events, row_plan, row_blocks, neg_share, neg_plan, neg_blocks
    )
    grad_terms, dx_pieces, x_lists, tabled = join(grad_terms, dx_pieces, x_lists, tabled)
    table_sum, bias_sum = tabled
    grad_near = dp_near(seal(units, grad_terms), True)
    dx_plan, dx_blocks = dp_cores(dx_plan, dx_pieces)
    scattered = scatter(units, items, x_lists, events, dx_plan, dx_blocks)
    grad_near, scattered = join(grad_near, scattered)
    (embed_sum,) = scattered
    grad_plan, grad_blocks = dp_cores(*dp_far(grad_near))
    in_sum, hid_sum, gate_sum, cand_sum, loss_sum = outputs(
        units, mp, dp, order_dp, grad_plan, grad_blocks
    )
    return (
        loss_sum[0, 0],
        in_sum,
        hid_sum,
        gate_sum,
        cand_sum.reshape(units),
        embed_sum,
        table_sum,
        bias_sum.reshape(items),
    )


def solution(mesh):
    return jax.shard_map(
        on_device,
        mesh=mesh,
        in_specs=(
            P(None, "dp"),
            P(None, "dp"),
            P(),
            P("mp", None),
            P(None, None, "mp"),
            P(None, None, "mp"),
            P(None, "mp"),
            P("mp"),
            P("mp", None),
            P(),
        ),
        out_specs=(
            P(),
            P(None, None, "mp"),
            P(None, None, "mp"),
            P(None, "mp"),
            P("mp"),
            P("mp", "dp"),
            P("mp", "dp"),
            P("dp"),
        ),
        check_vma=False,
    )
```
